32 devices in a mesh: groups: 2 (over y), seq: 4 (over z), head: 2 (over x), rep: 2 (over core).
Axes of the slice: x: 2, y: 2, z: 4, core: 2. Of those that a mesh axis runs over, the one named last changes fastest.
Arguments:
- normed: bfloat16 [2048, 4096], P(('groups', 'seq')), parts along dimension 0, may hold values from -6 to 6
- query_proj: bfloat16 [2048, 2048], P(('groups', 'seq'), ('head', 'rep')), parts along dimension 0, may hold values from -3 to 3
- key_proj: bfloat16 [2048, 2048], P(('groups', 'seq'), ('head', 'rep')), parts along dimension 0, may hold values from -3 to 3
- value_proj: bfloat16 [2048, 2048], P(('groups', 'seq'), ('head', 'rep')), parts along dimension 0, may hold values from -6 to 6
- out_weight: bfloat16 [2048, 4096], P(('head', 'rep'), 'seq'), may hold values from -0.125 to 0.125
- value_probe: bfloat16 [8192, 2048], P(('groups', 'seq'), ('head', 'rep')), parts along dimension 0, may hold values from -0.09375 to 0.09375
- out_probe: bfloat16 [4096, 4096], P(('groups', 'head', 'rep'), 'seq'), parts along dimension 0, may hold values from -0.125 to 0.125
Outputs:
- value_curv: bfloat16 [8192, 2048], P(('groups', 'seq'), ('head', 'rep')), parts along dimension 0
- out_curv: bfloat16 [4096, 4096], P(('groups', 'head', 'rep'), 'seq'), parts along dimension 0
The draws below stay inside these ranges and needn't reach their ends.
There are 2 independent parts, one for each index of `groups`. The reference program is written for one: setup_inputs(seed, part) draws one part's arguments, and reference() takes and returns one part's arrays. A program takes and returns all parts, laid end to end along the dimension named above; an argument that names none is the same for every part. Nothing has to cross between parts.
All inputs are finite; a program needn't handle non-finite values.
Results may differ from the reference program's by a relative error of at most 0.018.
Values may be sent and summed in bfloat16 or wider, within the bound.
No kernel may reach another device: no remote copies, remote signals or barrier semaphores. Data moves between devices by JAX's collectives and lax.ppermute only.
A program may use at most 128 MiB of HBM per device.

```python
import jax
import jax.numpy as jnp
from jax import lax

D = 4096
DH = 64
HEADS = 32
HD = 2048
TOKENS = 1024
N_SEQ = 4
N_HEAD = 2
N_REP = 2


def base_rows(key):
    first_key = jax.random.fold_in(key, 0)
    return 0.5 * jax.random.truncated_normal(first_key, -6.0, 6.0, (TOKENS, HEADS, DH), jnp.float32)


def draw_query_proj(key, part):
    key = jax.random.fold_in(key, 11)
    values = base_rows(key)
    return values.reshape(TOKENS, HEADS * DH).astype(jnp.bfloat16)


def draw_key_proj(key, part):
    key = jax.random.fold_in(key, 12)
    values = base_rows(key)
    return values.reshape(TOKENS, HEADS * DH).astype(jnp.bfloat16)


def strengthened(result, key, source, target, parts, factor):
    owner, partner = [(jnp.arange(result.shape[dim]) // (result.shape[dim] // parts)).reshape([-1 if axis == dim else 1 for axis in range(result.ndim)]) for dim in (source, target)]
    chosen = jax.random.permutation(key, parts)[partner]
    strong = (owner == chosen) | (owner == (partner + parts // 2) % parts)
    return jnp.where(strong, factor * result, result)


def levels(rng, dims, cuts, low, largest):
    def one(axis_at, shards_of):
        heights = jax.random.uniform(jax.random.fold_in(jax.random.fold_in(rng, 6), axis_at), (shards_of,), jnp.float32, low / len(cuts), largest / len(cuts))
        return jnp.repeat(jnp.exp(heights), dims[axis_at] // shards_of).reshape((-1,) + (1,) * (len(dims) - axis_at - 1))

    loudness = one(*cuts[0])
    for cut in cuts[1:]:
        loudness = loudness * one(*cut)
    return loudness


def scatter_about(own_key, shape, spread, bound, pieces=(), dtype=jnp.bfloat16):
    drawn = jax.random.normal(own_key, shape, jnp.float32) * spread
    if len(pieces) > 0:
        drawn = levels(own_key, shape, pieces, -0.22, 0.18) * drawn
    return jnp.clip(drawn, min=-bound, max=bound).astype(dtype)


def noise_with(own_key, shape, width, bound, cuts, heavy, kind=jnp.bfloat16):
    array = width * jax.random.normal(own_key, shape, jnp.float32)
    if cuts:
        array = array * levels(own_key, shape, cuts, -0.22, 0.18)
    return jnp.clip(strengthened(array, jax.random.fold_in(own_key, 3), *heavy), -bound, bound).astype(kind)


def setup_inputs(seed: int = 0, part: int = 0) -> dict:
    key_of = jax.random.split(jax.random.key(seed), 8)
    part_splits = jax.random.split(jax.random.fold_in(key_of[7], part), 8)
    return {
        "normed": noise_with(part_splits[0], (TOKENS, D), 1.0, 6.0, ((0, 4),), (0, 1, 4, 2.0)),
        "query_proj": draw_query_proj(jax.random.fold_in(jax.random.fold_in(key_of[7], part), 71), part),
        "key_proj": draw_key_proj(jax.random.fold_in(jax.random.fold_in(key_of[7], part), 71), part),
        "value_proj": scatter_about(part_splits[3], (TOKENS, HD), 1.0, 6.0, ((0, 4), (1, 4))),
        "out_weight": scatter_about(key_of[4], (HD, D), HD ** -0.5, 0.125, ((0, 4), (1, 4))),
        "value_probe": scatter_about(part_splits[5], (D, HD), D ** -0.5, 0.09375, ((0, 4), (1, 4))),
        "out_probe": scatter_about(part_splits[6], (HD, D), HD ** -0.5, 0.125, ((0, 4), (1, 4))),
    }


def by_head(matrix):
    return matrix.reshape(TOKENS, HEADS, DH).transpose(1, 0, 2)


def from_head(stacked):
    return stacked.transpose(1, 0, 2).reshape(TOKENS, HEADS * DH)


def attend(inputs):
    query_head, key_head, value_head, tangent_head = inputs
    scores = jnp.dot(query_head, key_head.T, preferred_element_type=jnp.float32)
    row_lse = jax.nn.logsumexp(scores, axis=1)
    prob_rows = jnp.exp(scores - row_lse[:, None]).astype(jnp.bfloat16)
    attended = jnp.dot(prob_rows, value_head, preferred_element_type=jnp.float32).astype(jnp.bfloat16)
    attended_tan = jnp.dot(prob_rows, tangent_head, preferred_element_type=jnp.float32).astype(jnp.bfloat16)
    return attended, attended_tan, row_lse


def value_grad_head(inputs):
    query_head, key_head, grad_head, row_lse = inputs
    scores = jnp.dot(query_head, key_head.T, preferred_element_type=jnp.float32)
    prob_rows = jnp.exp(scores - row_lse[:, None]).astype(jnp.bfloat16)
    return jnp.dot(prob_rows.T, grad_head, preferred_element_type=jnp.float32).astype(jnp.bfloat16)


def block_sum(left_rows, right_rows, blocks):
    left_blocks = left_rows.reshape(blocks, -1, left_rows.shape[1])
    right_blocks = right_rows.reshape(blocks, -1, right_rows.shape[1])

    def add_block(running, block_pair):
        block_term = jnp.dot(block_pair[0].T, block_pair[1], preferred_element_type=jnp.float32).astype(jnp.bfloat16)
        block_term = lax.optimization_barrier(block_term)
        return running + block_term.astype(jnp.float32), None

    start_sum = jnp.zeros((left_rows.shape[1], right_rows.shape[1]), jnp.float32)
    running, _ = lax.scan(add_block, start_sum, (left_blocks, right_blocks))
    return running.astype(jnp.bfloat16)


def reference(normed, query_proj, key_proj, value_proj, out_weight, value_probe, out_probe):
    value_tangent = jnp.dot(normed, value_probe, preferred_element_type=jnp.float32).astype(jnp.bfloat16)
    attended, attended_tan, row_lse = lax.map(attend, (by_head(query_proj), by_head(key_proj), by_head(value_proj), by_head(value_tangent)))
    attended = from_head(attended)
    attended_tan = from_head(attended_tan)
    slab_count = N_HEAD * N_REP
    slab_cols = HEADS * DH // slab_count
    tan_slabs = attended_tan.reshape(TOKENS, slab_count, slab_cols).transpose(1, 0, 2)
    att_slabs = attended.reshape(TOKENS, slab_count, slab_cols).transpose(1, 0, 2)
    weight_slabs = out_weight.reshape(slab_count, slab_cols, D)
    probe_slabs = out_probe.reshape(slab_count, slab_cols, D)

    def add_slab(running, slab_data):
        tan_s, att_s, weight_s, probe_s = slab_data
        slab_term = jnp.dot(tan_s, weight_s, preferred_element_type=jnp.float32) + jnp.dot(att_s, probe_s, preferred_element_type=jnp.float32)
        slab_term = lax.optimization_barrier(slab_term.astype(jnp.bfloat16))
        return running + slab_term.astype(jnp.float32), None

    tangent_out, _ = lax.scan(add_slab, jnp.zeros((TOKENS, D), jnp.float32), (tan_slabs, att_slabs, weight_slabs, probe_slabs))
    tangent_out = tangent_out.astype(jnp.bfloat16)
    out_curv = block_sum(attended, tangent_out, N_SEQ)
    grad_out = jnp.dot(tangent_out, out_weight.T, preferred_element_type=jnp.float32).astype(jnp.bfloat16)
    value_grad = from_head(lax.map(value_grad_head, (by_head(query_proj), by_head(key_proj), by_head(grad_out), row_lse)))
    value_curv = block_sum(normed, value_grad, N_SEQ)
    return value_curv, out_curv
```

```python
import jax
import jax.numpy as jnp
from jax import lax
from jax.sharding import PartitionSpec as P

DH = 64


def swap(x, axis):
    return lax.ppermute(x, axis, [(0, 1), (1, 0)])


def in_order(own, other, at):
    return jnp.where(at == 0, jnp.concatenate([own, other]), jnp.concatenate([other, own]))


def to_heads(x):
    n = lax.axis_size("seq")
    rows, cols = x.shape
    blocks = x.reshape(rows, n, cols // n).transpose(1, 0, 2)
    return lax.all_to_all(blocks, "seq", 0, 0).reshape(n * rows, cols // n)


def scatter_sum(x):
    n = lax.axis_size("seq")
    rows, cols = x.shape
    blocks = x.astype(jnp.bfloat16).reshape(rows, n, cols // n).transpose(1, 0, 2)
    got = lax.all_to_all(blocks, "seq", 0, 0)
    return jnp.sum(got.astype(jnp.float32), axis=0).astype(jnp.bfloat16)


def gather_cols(x):
    n = lax.axis_size("seq")
    me = lax.axis_index("seq")
    full = jnp.zeros((x.shape[0], n * x.shape[1]), x.dtype)
    for k in range(n):
        block = x if k == 0 else lax.ppermute(x, "seq", [(i, (i + k) % n) for i in range(n)])
        full = lax.dynamic_update_slice(full, block, (0, lax.rem(me - k + n, n) * x.shape[1]))
    return full


def dot(spec, a, b):
    return jnp.einsum(spec, a, b, preferred_element_type=jnp.float32)


def by_heads(normed, query_proj, key_proj, value_proj, out_weight, value_probe, out_probe):
    n = lax.axis_size("seq")
    at_head, at_rep = lax.axis_index("head"), lax.axis_index("rep")
    tok, width = normed.shape
    quarter = tok // 4
    slab = width // n
    mine = lax.dynamic_slice(normed, ((at_head * 2 + at_rep) * quarter, 0), (quarter, width))
    got = lax.all_to_all(mine.reshape(quarter, n, slab).transpose(1, 0, 2), "seq", 0, 0)
    pair = in_order(got[None], swap(got, "head")[None], at_head)
    four = in_order(pair[None], swap(pair, "rep")[None], at_rep)
    feats = four.transpose(2, 1, 0, 3, 4).reshape(n * tok, slab)
    query, key, value = to_heads(query_proj), to_heads(key_proj), to_heads(value_proj)
    tokens, cols = query.shape
    heads = cols // DH
    tangent = scatter_sum(dot("td,dc->tc", feats, value_probe))

    def split(x):
        return x.reshape(tokens, heads, DH)

    scores = dot("qhd,khd->hqk", split(query), split(key))
    top = jnp.max(scores, axis=2, keepdims=True)
    row_lse = top + jnp.log(jnp.sum(jnp.exp(scores - top), axis=2, keepdims=True))
    probs = jnp.exp(scores - row_lse).astype(jnp.bfloat16)
    attended = dot("hqk,khd->qhd", probs, split(value)).reshape(tokens, cols).astype(jnp.bfloat16)
    attended_tan = dot("hqk,khd->qhd", probs, split(tangent)).reshape(tokens, cols).astype(jnp.bfloat16)
    att, att_tan = gather_cols(attended), gather_cols(attended_tan)
    term = (dot("tc,cd->td", att, out_probe) + dot("tc,cd->td", att_tan, out_weight)).astype(jnp.bfloat16)
    half = tokens // 2
    away = lax.dynamic_slice(term, ((1 - at_rep) * half, 0), (half, slab))
    home = lax.dynamic_slice(term, (at_rep * half, 0), (half, slab))
    two = (home.astype(jnp.float32) + swap(away, "rep").astype(jnp.float32)).astype(jnp.bfloat16)
    all4 = (two.astype(jnp.float32) + swap(two, "head").astype(jnp.float32)).astype(jnp.bfloat16)
    tangent_out = in_order(all4, swap(all4, "rep"), at_rep)
    out_curv = dot("tc,td->cd", att, tangent_out).astype(jnp.bfloat16)
    grad_out = scatter_sum(dot("td,cd->tc", tangent_out, out_weight))
    value_grad = dot("hqk,qhd->khd", probs, split(grad_out)).reshape(tokens, cols).astype(jnp.bfloat16)
    value_curv = dot("td,tc->dc", feats, gather_cols(value_grad)).astype(jnp.bfloat16)
    return value_curv, out_curv


def body(*args):
    cols = args[1].shape[1]
    n = lax.axis_size("seq")
    even = cols % (n * 128) == 0 and args[0].shape[0] % 64 == 0
    if even and lax.axis_size("head") == 2 and lax.axis_size("rep") == 2:
        return by_heads(*args)
    return by_tokens(*args)


def by_tokens(normed, query_proj, key_proj, value_proj, out_weight, value_probe, out_probe):
    tok_rows = normed.shape[0]
    col_count = query_proj.shape[1]
    local_heads = col_count // DH
    feature_cols = normed
    value_tangent = jnp.dot(
        feature_cols,
        lax.all_gather(value_probe, "seq", axis=0, tiled=True),
        preferred_element_type=jnp.float32,
    ).astype(jnp.bfloat16)
    query_heads = query_proj.reshape(tok_rows, local_heads, DH)
    run_max = jnp.full((tok_rows, local_heads), -1e30, jnp.float32)
    key_rows = lax.all_gather(key_proj, "seq", axis=0, tiled=True)
    value_rows = lax.all_gather(value_proj, "seq", axis=0, tiled=True)
    tangent_rows = lax.all_gather(value_tangent, "seq", axis=0, tiled=True)
    piece_rows = key_rows.shape[0]
    key_heads = key_rows.reshape(piece_rows, local_heads, DH)
    value_heads = value_rows.reshape(piece_rows, local_heads, DH)
    tangent_heads = tangent_rows.reshape(piece_rows, local_heads, DH)
    scores = jnp.einsum("qhd,khd->qhk", query_heads, key_heads, preferred_element_type=jnp.float32)
    next_max = jnp.maximum(run_max, jnp.max(scores, axis=2))
    exp_rows = jnp.exp(scores - next_max[:, :, None])
    run_sum = jnp.sum(exp_rows, axis=2)
    prob_bf = exp_rows.astype(jnp.bfloat16)
    accum_v = jnp.einsum("qhk,khd->qhd", prob_bf, value_heads, preferred_element_type=jnp.float32)
    accum_t = jnp.einsum("qhk,khd->qhd", prob_bf, tangent_heads, preferred_element_type=jnp.float32)
    run_max, run_sum, accum_v, accum_t = (next_max, run_sum, accum_v, accum_t)
    row_lse = run_max + jnp.log(run_sum)
    attended = (accum_v / run_sum[:, :, None]).reshape(tok_rows, col_count).astype(jnp.bfloat16)
    attended_tan = (accum_t / run_sum[:, :, None]).reshape(tok_rows, col_count).astype(jnp.bfloat16)
    weight_full, probe_full = (
        lax.all_gather(out_weight, "seq", axis=1, tiled=True),
        lax.all_gather(out_probe, "seq", axis=1, tiled=True),
    )
    partial_out = jnp.dot(attended_tan, weight_full, preferred_element_type=jnp.float32) + jnp.dot(
        attended, probe_full, preferred_element_type=jnp.float32
    )
    tangent_out = lax.psum(partial_out.astype(jnp.bfloat16), ("head", "rep"))
    out_term = jnp.einsum("tc,td->cd", attended, tangent_out, preferred_element_type=jnp.float32)
    out_curv = lax.psum_scatter(
        out_term.astype(jnp.bfloat16), "seq", scatter_dimension=1, tiled=True
    )
    grad_out = jnp.einsum(
        "td,cd->tc", tangent_out, weight_full, preferred_element_type=jnp.float32
    ).astype(jnp.bfloat16)
    grad_heads = grad_out.reshape(tok_rows, local_heads, DH)
    every_key = lax.all_gather(key_proj, "seq", axis=0, tiled=True)
    key_rows = every_key.reshape(tok_rows * lax.axis_size("seq"), local_heads, DH)
    scores = jnp.einsum("qhd,khd->qhk", query_heads, key_rows, preferred_element_type=jnp.float32)
    prob_bf = jnp.exp(scores - row_lse[:, :, None]).astype(jnp.bfloat16)
    value_grad = lax.psum_scatter(
        jnp.einsum("qhk,qhd->khd", prob_bf, grad_heads, preferred_element_type=jnp.float32)
        .reshape(tok_rows * lax.axis_size("seq"), col_count)
        .astype(jnp.bfloat16),
        "seq",
        scatter_dimension=0,
        tiled=True,
    )
    feature_cols = normed
    value_curv = lax.psum_scatter(
        jnp.einsum(
            "tr,tc->rc", feature_cols, value_grad, preferred_element_type=jnp.float32
        ).astype(jnp.bfloat16),
        "seq",
        scatter_dimension=0,
        tiled=True,
    )
    return (value_curv, out_curv)


def solution(mesh):
    in_specs = (
        P(("groups", "seq"), None),
        P(("groups", "seq"), ("head", "rep")),
        P(("groups", "seq"), ("head", "rep")),
        P(("groups", "seq"), ("head", "rep")),
        P(("head", "rep"), "seq"),
        P(("groups", "seq"), ("head", "rep")),
        P(("groups", "head", "rep"), "seq"),
    )
    out_specs = (P(("groups", "seq"), ("head", "rep")), P(("groups", "head", "rep"), "seq"))
    return jax.shard_map(body, mesh=mesh, in_specs=in_specs, out_specs=out_specs, check_vma=False)
```

```python
from functools import partial

import jax
import jax.numpy as jnp
from jax import lax
from jax.experimental import pallas as pl
from jax.experimental.pallas import tpu as pltpu
from jax.sharding import PartitionSpec as P

DH = 64


VMEM = pl.BlockSpec(memory_space=pltpu.VMEM)
HBM = pl.BlockSpec(memory_space=pltpu.HBM)
ANY = pl.BlockSpec(memory_space=pl.ANY)


class Chain:
    def __init__(self):
        self.last = None

    def __call__(self, kernel, outs, ins, scratch=(), in_specs=None, first=(), mib=1):
        specs = in_specs or [VMEM] * len(ins)
        out_specs = [HBM] * len(outs) if in_specs and HBM in in_specs and VMEM not in in_specs else [VMEM] * len(outs)
        count = len(ins)
        if self.last is not None:
            first = [*first, self.last]
        ins, specs = [*ins, *first], [*specs, *[ANY] * len(first)]

        def body(*refs):
            kernel(*refs[:count], *refs[len(ins) :])

        results = pl.pallas_call(
            body,
            out_shape=outs,
            in_specs=specs,
            out_specs=out_specs,
            scratch_shapes=list(scratch),
            compiler_params=pltpu.CompilerParams(vmem_limit_bytes=44 * 2**20),
            cost_estimate=pl.CostEstimate(flops=1, bytes_accessed=mib * 2**20, transcendentals=0),
            name=getattr(kernel, "func", kernel).__name__,
        )(*ins)
        self.last = results[0]
        return results


def bf(*shape):
    return jax.ShapeDtypeStruct(shape, jnp.bfloat16)


def dot(a, b, ca=1, cb=0):
    return lax.dot_general(a, b, (((ca,), (cb,)), ((), ())), preferred_element_type=jnp.float32)


def at(index, size):
    return pl.ds(pl.multiple_of(index * size, size), size)


def ahead(x, k):
    n = lax.axis_size("seq")
    return lax.ppermute(x, "seq", [(i, (i + k) % n) for i in range(n)])


def swap(x, axis):
    return lax.ppermute(x, axis, [(0, 1), (1, 0)])


def after(x, *first):
    return lax.optimization_barrier((x, *first))[0]


def pack(*refs):
    out = refs[-1]
    for j, piece in enumerate(refs[:-1]):
        out[j] = piece[...]


def tangent_term(n, own, packed, peer, probe, feats, *refs):
    outs, whole = refs[:n], refs[n]
    me, head, rep = lax.axis_index("seq"), lax.axis_index("head"), lax.axis_index("rep")
    tok = own.shape[0]
    part = packed.shape[1]
    cols = outs[0].shape[1]
    for k in range(n):
        block = lax.rem(me - k + n, n)
        if k == 0:
            feats[at(block, tok), :] = own[...]
        else:
            for rows, core in ((packed, rep), (peer, 1 - rep)):
                for row, side in ((k - 1, head), (n - 2 + k, 1 - head)):
                    start = block * tok + (core * 2 + side) * part
                    feats[pl.ds(pl.multiple_of(start, part), part), :] = rows[row]
        whole[at(block, tok), :] = dot(feats[at(block, tok), :], probe[...]).astype(jnp.bfloat16)
    for k in range(n):
        outs[k][...] = whole[:, at(lax.rem(me + k, n), cols)]


def flip(feats, out):
    out[...] = feats[...].T


def keep_heads(parts):
    return jnp.concatenate([part[h * DH : (h + 1) * DH] for h, part in enumerate(parts)], axis=0)


def attend(n, *refs):
    own, pieces, (probs, attended, home, away, *all3) = refs[:3], refs[3 : n + 2], refs[n + 2 :]
    q_all, k_all, v_all = all3
    me = lax.axis_index("seq")
    tok, cols = pieces[0].shape[1:]
    for j in range(3):
        all3[j][at(me, tok), :] = own[j][:, at(me, cols)]
        for k in range(1, n):
            all3[j][at(lax.rem(me - k + n, n), tok), :] = pieces[k - 1][j]
    heads = cols // DH
    v_flip = v_all[...].T
    lane = lax.broadcasted_iota(jnp.int32, (tok, cols), 1) // DH

    @pl.loop(0, n)
    def _(c):
        rows = at(c, tok)
        parts = []
        for h in range(heads):
            query = jnp.where(lane == h, q_all[rows, :], 0)
            scores = dot(k_all[...], query, 1, 1)
            exps = jnp.exp(scores - jnp.max(scores, axis=0, keepdims=True))
            prob = (exps * (1.0 / jnp.sum(exps, axis=0, keepdims=True))).astype(jnp.bfloat16)
            probs[h, :, rows] = prob
            parts.append(dot(v_flip, prob))
        attended[rows, :] = keep_heads(parts).T.astype(jnp.bfloat16)

    halves(attended, home, away)


def halves(rows, home, away):
    head = lax.axis_index("head")
    half = home.shape[0]
    home[...] = rows[at(head, half), :]
    away[...] = rows[at(1 - head, half), :]


def attend_tan(n, *refs):
    terms, probs, (home, away, held, result, sems) = refs[:n], refs[n], refs[n + 1 :]
    heads = probs.shape[0]
    copies = [pltpu.make_async_copy(probs.at[h], held.at[h], sems.at[h]) for h in range(heads)]
    for copy in copies:
        copy.start()
    total = terms[0][...].astype(jnp.float32)
    for term in terms[1:]:
        total = total + term[...].astype(jnp.float32)
    flipped = total.T.astype(jnp.bfloat16)
    parts = []
    for h in range(heads):
        copies[h].wait()
        parts.append(dot(flipped, held[h]))
    result[...] = keep_heads(parts).T.astype(jnp.bfloat16)
    halves(result, home, away)


def add(one, two, out):
    out[...] = (one[...].astype(jnp.float32) + two[...].astype(jnp.float32)).astype(jnp.bfloat16)


def join(home, other, out):
    cols = home.shape[1]
    out[:, :cols] = home[...]
    out[:, cols:] = other[...]


def both_columns(n, pieces, lhs):
    me = lax.axis_index("seq")
    cols = pieces[0].shape[1] // 2
    for k in range(n):
        where = at(lax.rem(me - k + n, n), cols)
        for d in range(2):
            lhs[d, :, where] = pieces[k][:, d * cols : (d + 1) * cols]


def out_term(n, *refs):
    pieces, (probe, other, total, theirs, lhs) = refs[:n], refs[n:]
    both_columns(n, pieces, lhs)
    total[...] = dot(lhs[0], probe[...])
    total[...] += dot(lhs[1], other[...])
    theirs[...] = lhs[1]


def out_sum(n, *refs):
    base, pieces, weight, other, out, lhs = refs[0], refs[1 : n + 1], refs[n + 1], refs[n + 2], refs[n + 3], refs[n + 4]
    both_columns(n, pieces, lhs)
    total = base[...] + dot(lhs[0], weight[...])
    out[...] = (total + dot(lhs[1], other[...])).astype(jnp.bfloat16)


def grad_term(n, mine, other_core, weight, other, tangent_out, share, *refs):
    outs, grad = refs[:n], refs[n]
    me = lax.axis_index("seq")
    cols = outs[0].shape[1] // 2
    tangent_out[...] = (mine[...].astype(jnp.float32) + other_core[...].astype(jnp.float32)).astype(jnp.bfloat16)
    share[...] = tangent_out[at(lax.axis_index("rep"), share.shape[0]), :]
    for d, rows in enumerate((weight, other)):
        grad[d] = dot(tangent_out[...], rows[...], 1, 1).astype(jnp.bfloat16)
        for k in range(n):
            outs[k][:, d * cols : (d + 1) * cols] = grad[d, :, at(lax.rem(me + k, n), cols)]


def add_grad(n, *refs):
    terms, home, away = refs[:n], refs[n], refs[n + 1]
    total = terms[0][...].astype(jnp.float32)
    for term in terms[1:]:
        total = total + term[...].astype(jnp.float32)
    cols = home.shape[1]
    home[...] = total[:, :cols].astype(jnp.bfloat16)
    away[...] = total[:, cols:].astype(jnp.bfloat16)


def key_grad(mine, theirs, probs, out, grad, held, sems):
    heads, tokens, _ = probs.shape
    half, cols = mine.shape
    parts = held.shape[0]
    rows = tokens // parts
    copies = [pltpu.make_async_copy(probs.at[:, pl.ds(c * rows, rows)], held.at[c], sems.at[c]) for c in range(parts)]
    for copy in copies:
        copy.start()
    head = lax.axis_index("head")
    grad[at(head, half), :] = mine[...]
    grad[at(1 - head, half), :] = theirs[...]
    lane = lax.broadcasted_iota(jnp.int32, (rows, cols), 1) // DH
    for c in range(parts):
        copies[c].wait()
        value = dot(held[c, 0], grad[...])
        for h in range(1, heads):
            value = jnp.where(lane == h, dot(held[c, h], grad[...]), value)
        out[pl.ds(c * rows, rows), :] = value.astype(jnp.bfloat16)


def value_product(n, *refs):
    flipped, blocks, out, rhs = refs[0], refs[1 : n + 1], refs[n + 1], refs[n + 2]
    me = lax.axis_index("seq")
    cols = blocks[0].shape[1]
    for k in range(n):
        rhs[:, at(lax.rem(me - k + n, n), cols)] = blocks[k][...]
    out[...] = dot(flipped[...], rhs[...]).astype(jnp.bfloat16)


def out_product(n, *refs):
    pieces, (theirs, mine, one, two, out, other) = refs[:n], refs[n:]
    me, rep = lax.axis_index("seq"), lax.axis_index("rep")
    cols = pieces[0].shape[1] // 2
    other[at(rep, one.shape[0]), :] = one[...]
    other[at(1 - rep, one.shape[0]), :] = two[...]
    for k in range(n):
        where = at(lax.rem(me - k + n, n), cols)
        total = dot(pieces[k][:, :cols].T, mine[...])
        out[where, :] = (total + dot(theirs[:, where].T, other[...])).astype(jnp.bfloat16)


def by_heads(normed, query_proj, key_proj, value_proj, out_weight, value_probe, out_probe):
    n = lax.axis_size("seq")
    me, head, rep = lax.axis_index("seq"), lax.axis_index("head"), lax.axis_index("rep")
    tok, width = normed.shape
    block = query_proj.shape[1]
    slab, cols, tokens = width // n, block // n, tok * n
    half, heads = tokens // 2, block // n // DH
    call = Chain()
    part = partial
    dma = pltpu.SemaphoreType.DMA
    f32 = jnp.float32

    def held(*shape):
        return pltpu.VMEM(shape, jnp.bfloat16)

    def gathered(x):
        pieces = [x] + [None] * (n - 1)
        for k in range(1, (n - 1) // 2 + 1):
            pieces[k] = ahead(pieces[k - 1], 1)
        for k in range(1, n // 2 + 1):
            pieces[n - k] = ahead(pieces[(n - k + 1) % n], n - 1)
        return pieces

    def summed(terms):
        sums = [terms[0]]
        for step, far in ((1, n // 2), (-1, (n - 1) // 2)):
            total = ahead(terms[step * far], step)
            for k in range(far - 1, 0, -1):
                (total,) = call(add, [bf(*total.shape)], [total, terms[step * k]])
                total = ahead(total, step)
            sums.append(total)
        return sums

    quarter = tok // 4
    start = (rep * 2 + head) * quarter
    got = [
        ahead(lax.dynamic_slice(normed, (start, lax.rem(me + k, n) * slab), (quarter, slab)), k) for k in range(1, n)]
    own = lax.dynamic_slice(normed, (0, me * slab), (tok, slab))
    proj = (query_proj, key_proj, value_proj)
    qkv = []
    for k in range(1, n):
        piece = jnp.stack([lax.dynamic_slice(x, (0, lax.rem(me + k, n) * cols), (tok, cols)) for x in proj])
        qkv.append(ahead(piece, k))
    other = [swap(x, "head") for x in got]
    (packed,) = call(pack, [bf(2 * (n - 1), quarter, slab)], [*got, *other], first=qkv)
    feats, *terms = call(
        part(tangent_term, n), [bf(tokens, slab)] + [bf(tokens, cols)] * n,
        [own, packed, swap(packed, "rep"), value_probe], scratch=[held(tokens, block)])
    probs, _, home, away = call(
        part(attend, n), [bf(heads, tokens, tokens), bf(tokens, cols)] + [bf(half, cols)] * 2, [*proj, *qkv],
        scratch=[held(tokens, cols)] * 3, mib=32)
    away = swap(away, "head")
    tangent = summed(terms)
    other_probe = swap(after(out_probe, feats), "head")
    tan, tan_away = call(
        part(attend_tan, 3), [bf(half, cols)] * 2, [*tangent, probs],
        scratch=[held(heads, tokens, tokens), held(tokens, cols), dma((heads,))], in_specs=[VMEM] * 3 + [ANY])
    (att,) = call(join, [bf(half, 2 * cols)], [home, away])
    att = gathered(att)
    (tan,) = call(join, [bf(half, 2 * cols)], [tan, swap(after(tan_away, att[0]), "head")], first=[att[1], att[-1]])
    other_weight = swap(after(out_weight, tan), "head")
    tan = gathered(tan)
    base, theirs = call(
        part(out_term, n), [jax.ShapeDtypeStruct((half, slab), f32), bf(half, block)], [*att, out_probe, other_probe],
        scratch=[held(2, half, block)])
    (mine,) = call(
        part(out_sum, n), [bf(half, slab)], [base, *tan, out_weight, other_weight], scratch=[held(2, half, block)])
    tangent_out, share, *grads = call(
        part(grad_term, n), [bf(half, slab), bf(half // 2, slab)] + [bf(half, 2 * cols)] * n,
        [mine, swap(mine, "rep"), out_weight, other_weight],
        scratch=[held(2, half, block)])
    home, away = call(part(add_grad, 3), [bf(half, cols)] * 2, summed(grads))
    (value_grad,) = call(
        key_grad, [bf(tokens, cols)], [home, swap(away, "head"), probs],
        scratch=[held(tokens, cols), held(4, heads, tokens // 4, tokens), dma((4,))], in_specs=[VMEM] * 2 + [ANY])
    value_grad = gathered(value_grad)
    share = swap(share, "head")
    (out_curv,) = call(
        part(out_product, n), [bf(block, slab)], [*att, swap(theirs, "head"), tangent_out, share, swap(share, "rep")],
        scratch=[held(half, slab)])
    (flipped,) = call(flip, [bf(slab, tokens)], [feats])
    (value_curv,) = call(
        part(value_product, n), [bf(slab, block)], [flipped, *value_grad], scratch=[held(tokens, block)])
    return value_curv, out_curv


def body(*args):
    tok, cols = args[1].shape
    n = lax.axis_size("seq")
    even = cols % (n * 128) == 0 and tok % 64 == 0 and tok * n % 64 == 0
    if even and lax.axis_size("head") == 2 and lax.axis_size("rep") == 2:
        return by_heads(*args)
    return by_tokens(*args)


def by_tokens(normed, query_proj, key_proj, value_proj, out_weight, value_probe, out_probe):
    tok_rows = normed.shape[0]
    col_count = query_proj.shape[1]
    local_heads = col_count // DH
    feature_cols = normed
    value_tangent = jnp.dot(
        feature_cols,
        lax.all_gather(value_probe, "seq", axis=0, tiled=True),
        preferred_element_type=jnp.float32,
    ).astype(jnp.bfloat16)
    query_heads = query_proj.reshape(tok_rows, local_heads, DH)
    run_max = jnp.full((tok_rows, local_heads), -1e30, jnp.float32)
    key_rows = lax.all_gather(key_proj, "seq", axis=0, tiled=True)
    value_rows = lax.all_gather(value_proj, "seq", axis=0, tiled=True)
    tangent_rows = lax.all_gather(value_tangent, "seq", axis=0, tiled=True)
    piece_rows = key_rows.shape[0]
    key_heads = key_rows.reshape(piece_rows, local_heads, DH)
    value_heads = value_rows.reshape(piece_rows, local_heads, DH)
    tangent_heads = tangent_rows.reshape(piece_rows, local_heads, DH)
    scores = jnp.einsum("qhd,khd->qhk", query_heads, key_heads, preferred_element_type=jnp.float32)
    next_max = jnp.maximum(run_max, jnp.max(scores, axis=2))
    exp_rows = jnp.exp(scores - next_max[:, :, None])
    run_sum = jnp.sum(exp_rows, axis=2)
    prob_bf = exp_rows.astype(jnp.bfloat16)
    accum_v = jnp.einsum("qhk,khd->qhd", prob_bf, value_heads, preferred_element_type=jnp.float32)
    accum_t = jnp.einsum("qhk,khd->qhd", prob_bf, tangent_heads, preferred_element_type=jnp.float32)
    run_max, run_sum, accum_v, accum_t = (next_max, run_sum, accum_v, accum_t)
    row_lse = run_max + jnp.log(run_sum)
    attended = (accum_v / run_sum[:, :, None]).reshape(tok_rows, col_count).astype(jnp.bfloat16)
    attended_tan = (accum_t / run_sum[:, :, None]).reshape(tok_rows, col_count).astype(jnp.bfloat16)
    weight_full, probe_full = (
        lax.all_gather(out_weight, "seq", axis=1, tiled=True),
        lax.all_gather(out_probe, "seq", axis=1, tiled=True),
    )
    partial_out = jnp.dot(attended_tan, weight_full, preferred_element_type=jnp.float32) + jnp.dot(
        attended, probe_full, preferred_element_type=jnp.float32
    )
    tangent_out = lax.psum(partial_out.astype(jnp.bfloat16), ("head", "rep"))
    out_term = jnp.einsum("tc,td->cd", attended, tangent_out, preferred_element_type=jnp.float32)
    out_curv = lax.psum_scatter(
        out_term.astype(jnp.bfloat16), "seq", scatter_dimension=1, tiled=True
    )
    grad_out = jnp.einsum(
        "td,cd->tc", tangent_out, weight_full, preferred_element_type=jnp.float32
    ).astype(jnp.bfloat16)
    grad_heads = grad_out.reshape(tok_rows, local_heads, DH)
    every_key = lax.all_gather(key_proj, "seq", axis=0, tiled=True)
    key_rows = every_key.reshape(tok_rows * lax.axis_size("seq"), local_heads, DH)
    scores = jnp.einsum("qhd,khd->qhk", query_heads, key_rows, preferred_element_type=jnp.float32)
    prob_bf = jnp.exp(scores - row_lse[:, :, None]).astype(jnp.bfloat16)
    value_grad = lax.psum_scatter(
        jnp.einsum("qhk,qhd->khd", prob_bf, grad_heads, preferred_element_type=jnp.float32)
        .reshape(tok_rows * lax.axis_size("seq"), col_count)
        .astype(jnp.bfloat16),
        "seq",
        scatter_dimension=0,
        tiled=True,
    )
    feature_cols = normed
    value_curv = lax.psum_scatter(
        jnp.einsum(
            "tr,tc->rc", feature_cols, value_grad, preferred_element_type=jnp.float32
        ).astype(jnp.bfloat16),
        "seq",
        scatter_dimension=0,
        tiled=True,
    )
    return (value_curv, out_curv)


def solution(mesh):
    in_specs = (
        P(("groups", "seq"), None),
        P(("groups", "seq"), ("head", "rep")),
        P(("groups", "seq"), ("head", "rep")),
        P(("groups", "seq"), ("head", "rep")),
        P(("head", "rep"), "seq"),
        P(("groups", "seq"), ("head", "rep")),
        P(("groups", "head", "rep"), "seq"),
    )
    out_specs = (P(("groups", "seq"), ("head", "rep")), P(("groups", "head", "rep"), "seq"))
    return jax.shard_map(body, mesh=mesh, in_specs=in_specs, out_specs=out_specs, check_vma=False)
```

```python
from functools import partial

import jax
import jax.numpy as jnp
from jax import lax
from jax.experimental import pallas as pl
from jax.experimental.pallas import tpu as pltpu
from jax.sharding import PartitionSpec as P

DH = 64


VMEM = pl.BlockSpec(memory_space=pltpu.VMEM)
HBM = pl.BlockSpec(memory_space=pltpu.HBM)
ANY = pl.BlockSpec(memory_space=pl.ANY)


class Chain:
    def __init__(self):
        self.last = None

    def __call__(self, kernel, outs, ins, scratch=(), in_specs=None, first=()):
        specs = in_specs or [VMEM] * len(ins)
        out_specs = [HBM] * len(outs) if in_specs and HBM in in_specs and VMEM not in in_specs else [VMEM] * len(outs)
        count = len(ins)
        if self.last is not None:
            first = [*first, self.last]
        ins, specs = [*ins, *first], [*specs, *[ANY] * len(first)]

        def body(*refs):
            kernel(*refs[:count], *refs[len(ins) :])

        results = pl.pallas_call(
            body,
            out_shape=outs,
            in_specs=specs,
            out_specs=out_specs,
            scratch_shapes=list(scratch),
            compiler_params=pltpu.CompilerParams(vmem_limit_bytes=18 * 2**20),
            cost_estimate=pl.CostEstimate(flops=1, bytes_accessed=1, transcendentals=0),
            name=getattr(kernel, "func", kernel).__name__,
        )(*ins)
        self.last = results[0]
        return results


def bf(*shape):
    return jax.ShapeDtypeStruct(shape, jnp.bfloat16)


def dot(a, b, ca=1, cb=0):
    return lax.dot_general(a, b, (((ca,), (cb,)), ((), ())), preferred_element_type=jnp.float32)


def at(index, size):
    return pl.ds(pl.multiple_of(index * size, size), size)


def ahead(x, k):
    n = lax.axis_size("seq")
    return lax.ppermute(x, "seq", [(i, (i + k) % n) for i in range(n)])


def swap(x, axis):
    return lax.ppermute(x, axis, [(0, 1), (1, 0)])


def after(x, *first):
    return lax.optimization_barrier((x, *first))[0]


def pack(*refs):
    *pieces, weight, out, share, sem = refs
    copy = pltpu.make_async_copy(weight.at[at(lax.axis_index("groups"), share.shape[0])], share, sem)
    copy.start()
    for j, piece in enumerate(pieces):
        out[j] = piece[...]
    copy.wait()


def tangent_term(n, normed, packed, peer, probe, feats, *refs):
    outs, whole, sem = refs[:n], refs[n], refs[n + 1]
    me, head, rep = lax.axis_index("seq"), lax.axis_index("head"), lax.axis_index("rep")
    tok = normed.shape[0]
    part, slab = packed.shape[1:]
    copy = pltpu.make_async_copy(normed.at[:, at(me, slab)], feats.at[at(me, tok)], sem)
    copy.start()
    cols = outs[0].shape[1]
    for k in [*range(1, n), 0]:
        block = lax.rem(me - k + n, n)
        if k == 0:
            copy.wait()
        else:
            for rows, core in ((packed, rep), (peer, 1 - rep)):
                for row, side in ((k % (n - 1), head), (n - 1 + k % (n - 1), 1 - head)):
                    start = block * tok + (core * 2 + side) * part
                    feats[pl.ds(pl.multiple_of(start, part), part), :] = rows[row]
        whole[at(block, tok), :] = dot(feats[at(block, tok), :], probe[...]).astype(jnp.bfloat16)
    for k in range(n):
        outs[k][...] = whole[:, at(lax.rem(me + k, n), cols)]


def flip(feats, out):
    out[...] = feats[...].T


def keep_heads(parts):
    return jnp.concatenate([part[h * DH : (h + 1) * DH] for h, part in enumerate(parts)], axis=0)


def attend(n, *refs):
    own, pieces, (probs, attended, *all3) = refs[:3], refs[3 : n + 2], refs[n + 2 :]
    q_all, k_all, v_all = all3
    me = lax.axis_index("seq")
    tok, cols = pieces[0].shape[1:]
    for j in range(3):
        all3[j][at(me, tok), :] = own[j][:, at(me, cols)]
        for k in range(1, n):
            all3[j][at(lax.rem(me - k + n, n), tok), :] = pieces[k - 1][j]
    heads = cols // DH
    v_flip = v_all[...].T
    lane = lax.broadcasted_iota(jnp.int32, (tok, cols), 1) // DH

    @pl.loop(0, n)
    def _(c):
        rows = at(c, tok)
        parts = []
        for h in range(heads):
            query = jnp.where(lane == h, q_all[rows, :], 0)
            scores = dot(k_all[...], query, 1, 1)
            exps = jnp.exp(scores - jnp.max(scores, axis=0, keepdims=True))
            prob = (exps * (1.0 / jnp.sum(exps, axis=0, keepdims=True))).astype(jnp.bfloat16)
            probs[h, :, rows] = prob
            parts.append(dot(v_flip, prob))
        attended[rows, :] = keep_heads(parts).T.astype(jnp.bfloat16)


def halves(rows, home, away):
    head = lax.axis_index("head")
    half = home.shape[0]
    home[...] = rows[at(head, half), :]
    away[...] = rows[at(1 - head, half), :]


def attend_tan(n, *refs):
    terms, probs, (home, away, held, result, sems) = refs[:n], refs[n], refs[n + 1 :]
    heads = probs.shape[0]
    copies = [pltpu.make_async_copy(probs.at[h], held.at[h], sems.at[h]) for h in range(heads)]
    for copy in copies:
        copy.start()
    total = terms[0][...].astype(jnp.float32)
    for term in terms[1:]:
        total = total + term[...].astype(jnp.float32)
    flipped = total.T.astype(jnp.bfloat16)
    parts = []
    for h in range(heads):
        copies[h].wait()
        parts.append(dot(flipped, held[h]))
    result[...] = keep_heads(parts).T.astype(jnp.bfloat16)
    halves(result, home, away)


def add(one, two, out):
    out[...] = (one[...].astype(jnp.float32) + two[...].astype(jnp.float32)).astype(jnp.bfloat16)


def join(home, other, out):
    cols = home.shape[1]
    out[:, :cols] = home[...]
    out[:, cols:] = other[...]


def cut_rows(n, *refs):
    pieces, away = refs[:n], refs[n]
    me, head = lax.axis_index("seq"), lax.axis_index("head")
    half = away.shape[0]
    cols = pieces[0].shape[1]
    for k in range(n):
        away[:, at(lax.rem(me - k + n, n), cols)] = pieces[k][at(1 - head, half), :]


def out_term(n, *refs):
    pieces, (theirs, probe, other, total, lhs) = refs[:n], refs[n:]
    me, head = lax.axis_index("seq"), lax.axis_index("head")
    half = theirs.shape[0]
    cols = pieces[0].shape[1]
    for k in range(n):
        lhs[:, at(lax.rem(me - k + n, n), cols)] = pieces[k][at(head, half), :]
    total[...] = dot(lhs[...], probe[...])
    total[...] += dot(theirs[...], other[...])


def out_sum(n, *refs):
    base, pieces, (weight, one, two, out, lhs) = refs[0], refs[1 : n + 1], refs[n + 1 :]
    me, group = lax.axis_index("seq"), lax.axis_index("groups")
    cols = pieces[0].shape[1] // 2
    for k in range(n):
        where = at(lax.rem(me - k + n, n), cols)
        for d in range(2):
            lhs[d, :, where] = pieces[k][:, d * cols : (d + 1) * cols]
    rows = one.shape[0]
    total = base[...] + dot(lhs[0], weight[...])
    total = total + dot(lhs[1, :, at(group, rows)], one[...])
    out[...] = (total + dot(lhs[1, :, at(1 - group, rows)], two[...])).astype(jnp.bfloat16)


def grad_term(n, mine, other_core, weight, one, two, tangent_out, share, *refs):
    outs, grad = refs[:n], refs[n]
    me = lax.axis_index("seq")
    cols = outs[0].shape[1] // 2
    tangent_out[...] = (mine[...].astype(jnp.float32) + other_core[...].astype(jnp.float32)).astype(jnp.bfloat16)
    share[...] = tangent_out[at(lax.axis_index("rep"), share.shape[0]), :]
    group = lax.axis_index("groups")
    rows = one.shape[0]
    grad[0] = dot(tangent_out[...], weight[...], 1, 1).astype(jnp.bfloat16)
    grad[1, :, at(group, rows)] = dot(tangent_out[...], one[...], 1, 1).astype(jnp.bfloat16)
    grad[1, :, at(1 - group, rows)] = dot(tangent_out[...], two[...], 1, 1).astype(jnp.bfloat16)
    for d in range(2):
        for k in range(n):
            outs[k][:, d * cols : (d + 1) * cols] = grad[d, :, at(lax.rem(me + k, n), cols)]


def add_grad(n, *refs):
    terms, home, away = refs[:n], refs[n], refs[n + 1]
    total = terms[0][...].astype(jnp.float32)
    for term in terms[1:]:
        total = total + term[...].astype(jnp.float32)
    cols = home.shape[1]
    home[...] = total[:, :cols].astype(jnp.bfloat16)
    away[...] = total[:, cols:].astype(jnp.bfloat16)


def key_grad(mine, theirs, probs, out, grad, held, sems):
    heads, tokens, _ = probs.shape
    half, cols = mine.shape
    parts = held.shape[0]
    rows = tokens // parts
    copies = [pltpu.make_async_copy(probs.at[:, pl.ds(c * rows, rows)], held.at[c], sems.at[c]) for c in range(parts)]
    for copy in copies:
        copy.start()
    head = lax.axis_index("head")
    grad[at(head, half), :] = mine[...]
    grad[at(1 - head, half), :] = theirs[...]
    lane = lax.broadcasted_iota(jnp.int32, (rows, cols), 1) // DH
    for c in range(parts):
        copies[c].wait()
        value = dot(held[c, 0], grad[...])
        for h in range(1, heads):
            value = jnp.where(lane == h, dot(held[c, h], grad[...]), value)
        out[pl.ds(c * rows, rows), :] = value.astype(jnp.bfloat16)


def value_product(n, *refs):
    flipped, blocks, out, rhs = refs[0], refs[1 : n + 1], refs[n + 1], refs[n + 2]
    me = lax.axis_index("seq")
    cols = blocks[0].shape[1]
    for k in range(n):
        rhs[:, at(lax.rem(me - k + n, n), cols)] = blocks[k][...]
    out[...] = dot(flipped[...], rhs[...]).astype(jnp.bfloat16)


def out_product(n, *refs):
    pieces, (mine, one, two, out, rows) = refs[:n], refs[n:]
    me, head, rep = lax.axis_index("seq"), lax.axis_index("head"), lax.axis_index("rep")
    cols = pieces[0].shape[1]
    half, part = mine.shape[0], one.shape[0]
    rows[at(head, half), :] = mine[...]
    for index, piece in ((rep, one), (1 - rep, two)):
        start = (1 - head) * half + index * part
        rows[pl.ds(pl.multiple_of(start, part), part), :] = piece[...]
    for k in range(n):
        out[at(lax.rem(me - k + n, n), cols), :] = dot(pieces[k][...].T, rows[...]).astype(jnp.bfloat16)


def by_heads(normed, query_proj, key_proj, value_proj, out_weight, value_probe, out_probe):
    n = lax.axis_size("seq")
    me, head, rep = lax.axis_index("seq"), lax.axis_index("head"), lax.axis_index("rep")
    tok, width = normed.shape
    block = query_proj.shape[1]
    slab, cols, tokens = width // n, block // n, tok * n
    half, heads = tokens // 2, block // n // DH
    call = Chain()
    part = partial
    dma = pltpu.SemaphoreType.DMA
    f32 = jnp.float32

    def held(*shape):
        return pltpu.VMEM(shape, jnp.bfloat16)

    def gathered(x):
        pieces = [x] + [None] * (n - 1)
        for k in range(1, (n - 1) // 2 + 1):
            pieces[k] = ahead(pieces[k - 1], 1)
        for k in range(1, n // 2 + 1):
            pieces[n - k] = ahead(pieces[(n - k + 1) % n], n - 1)
        return pieces

    def summed(terms):
        sums = [terms[0]]
        for step, far in ((1, n // 2), (-1, (n - 1) // 2)):
            total = ahead(terms[step * far], step)
            for k in range(far - 1, 0, -1):
                (total,) = call(add, [bf(*total.shape)], [total, terms[step * k]])
                total = ahead(total, step)
            sums.append(total)
        return sums

    quarter = tok // 4
    start = (rep * 2 + head) * quarter
    got = [
        ahead(lax.dynamic_slice(normed, (start, lax.rem(me + k, n) * slab), (quarter, slab)), k) for k in range(1, n)]
    proj = (query_proj, key_proj, value_proj)
    qkv = []
    for k in range(1, n):
        piece = jnp.stack([lax.dynamic_slice(x, (0, lax.rem(me + k, n) * cols), (tok, cols)) for x in proj])
        qkv.append(ahead(after(piece, got[0]), k))
    got = got[-1:] + got[:-1]
    other = [swap(x, "head") for x in got]
    packed, share = call(
        pack, [bf(2 * (n - 1), quarter, slab), bf(block // 2, slab)], [*got, *other, out_weight],
        scratch=[dma(())], in_specs=[VMEM] * (2 * n - 2) + [ANY], first=qkv[:2])
    feats, *terms = call(
        part(tangent_term, n), [bf(tokens, slab)] + [bf(tokens, cols)] * n,
        [normed, packed, swap(packed, "rep"), value_probe], scratch=[held(tokens, block), dma(())],
        in_specs=[ANY] + [VMEM] * 3, first=qkv[2:])
    other_probe = swap(after(out_probe, packed), "head")
    weights = [swap(after(share, feats), "head")]
    probs, attended = call(
        part(attend, n), [bf(heads, tokens, tokens), bf(tokens, cols)], [*proj, *qkv],
        scratch=[held(tokens, cols)] * 3)
    att = gathered(attended)
    tangent = summed(terms)
    tan, tan_away = call(
        part(attend_tan, 3), [bf(half, cols)] * 2, [*tangent, probs],
        scratch=[held(heads, tokens, tokens), held(tokens, cols), dma((heads,))], in_specs=[VMEM] * 3 + [ANY])
    (tan,) = call(join, [bf(half, 2 * cols)], [tan, swap(tan_away, "head")], first=[att[1], att[-1]])
    weights.append(swap(weights[0], "groups"))
    tan = gathered(tan)
    (away,) = call(part(cut_rows, n), [bf(half, block)], att)
    (base,) = call(
        part(out_term, n), [jax.ShapeDtypeStruct((half, slab), f32)],
        [*att, swap(away, "head"), out_probe, other_probe], scratch=[held(half, block)])
    (mine,) = call(
        part(out_sum, n), [bf(half, slab)], [base, *tan, out_weight, *weights], scratch=[held(2, half, block)])
    tangent_out, share, *grads = call(
        part(grad_term, n), [bf(half, slab), bf(half // 2, slab)] + [bf(half, 2 * cols)] * n,
        [mine, swap(mine, "rep"), out_weight, *weights],
        scratch=[held(2, half, block)])
    home, away = call(part(add_grad, 3), [bf(half, cols)] * 2, summed(grads))
    (value_grad,) = call(
        key_grad, [bf(tokens, cols)], [home, swap(away, "head"), probs],
        scratch=[held(tokens, cols), held(4, heads, tokens // 4, tokens), dma((4,))], in_specs=[VMEM] * 2 + [ANY])
    value_grad = gathered(value_grad)
    share = swap(share, "head")
    (out_curv,) = call(
        part(out_product, n), [bf(block, slab)], [*att, tangent_out, share, swap(share, "rep")],
        scratch=[held(tokens, slab)])
    (flipped,) = call(flip, [bf(slab, tokens)], [feats])
    (value_curv,) = call(
        part(value_product, n), [bf(slab, block)], [flipped, *value_grad], scratch=[held(tokens, block)])
    return value_curv, out_curv


def body(*args):
    tok, cols = args[1].shape
    n = lax.axis_size("seq")
    even = cols % (n * 128) == 0 and tok % 64 == 0 and tok * n % 64 == 0
    if even and all(lax.axis_size(axis) == 2 for axis in ("groups", "head", "rep")):
        return by_heads(*args)
    return by_tokens(*args)


def by_tokens(normed, query_proj, key_proj, value_proj, out_weight, value_probe, out_probe):
    tok_rows = normed.shape[0]
    col_count = query_proj.shape[1]
    local_heads = col_count // DH
    feature_cols = normed
    value_tangent = jnp.dot(
        feature_cols,
        lax.all_gather(value_probe, "seq", axis=0, tiled=True),
        preferred_element_type=jnp.float32,
    ).astype(jnp.bfloat16)
    query_heads = query_proj.reshape(tok_rows, local_heads, DH)
    run_max = jnp.full((tok_rows, local_heads), -1e30, jnp.float32)
    key_rows = lax.all_gather(key_proj, "seq", axis=0, tiled=True)
    value_rows = lax.all_gather(value_proj, "seq", axis=0, tiled=True)
    tangent_rows = lax.all_gather(value_tangent, "seq", axis=0, tiled=True)
    piece_rows = key_rows.shape[0]
    key_heads = key_rows.reshape(piece_rows, local_heads, DH)
    value_heads = value_rows.reshape(piece_rows, local_heads, DH)
    tangent_heads = tangent_rows.reshape(piece_rows, local_heads, DH)
    scores = jnp.einsum("qhd,khd->qhk", query_heads, key_heads, preferred_element_type=jnp.float32)
    next_max = jnp.maximum(run_max, jnp.max(scores, axis=2))
    exp_rows = jnp.exp(scores - next_max[:, :, None])
    run_sum = jnp.sum(exp_rows, axis=2)
    prob_bf = exp_rows.astype(jnp.bfloat16)
    accum_v = jnp.einsum("qhk,khd->qhd", prob_bf, value_heads, preferred_element_type=jnp.float32)
    accum_t = jnp.einsum("qhk,khd->qhd", prob_bf, tangent_heads, preferred_element_type=jnp.float32)
    run_max, run_sum, accum_v, accum_t = (next_max, run_sum, accum_v, accum_t)
    row_lse = run_max + jnp.log(run_sum)
    attended = (accum_v / run_sum[:, :, None]).reshape(tok_rows, col_count).astype(jnp.bfloat16)
    attended_tan = (accum_t / run_sum[:, :, None]).reshape(tok_rows, col_count).astype(jnp.bfloat16)
    weight_full, probe_full = (
        lax.all_gather(out_weight, "seq", axis=1, tiled=True),
        lax.all_gather(out_probe, "seq", axis=1, tiled=True),
    )
    partial_out = jnp.dot(attended_tan, weight_full, preferred_element_type=jnp.float32) + jnp.dot(
        attended, probe_full, preferred_element_type=jnp.float32
    )
    tangent_out = lax.psum(partial_out.astype(jnp.bfloat16), ("head", "rep"))
    out_term = jnp.einsum("tc,td->cd", attended, tangent_out, preferred_element_type=jnp.float32)
    out_curv = lax.psum_scatter(
        out_term.astype(jnp.bfloat16), "seq", scatter_dimension=1, tiled=True
    )
    grad_out = jnp.einsum(
        "td,cd->tc", tangent_out, weight_full, preferred_element_type=jnp.float32
    ).astype(jnp.bfloat16)
    grad_heads = grad_out.reshape(tok_rows, local_heads, DH)
    every_key = lax.all_gather(key_proj, "seq", axis=0, tiled=True)
    key_rows = every_key.reshape(tok_rows * lax.axis_size("seq"), local_heads, DH)
    scores = jnp.einsum("qhd,khd->qhk", query_heads, key_rows, preferred_element_type=jnp.float32)
    prob_bf = jnp.exp(scores - row_lse[:, :, None]).astype(jnp.bfloat16)
    value_grad = lax.psum_scatter(
        jnp.einsum("qhk,qhd->khd", prob_bf, grad_heads, preferred_element_type=jnp.float32)
        .reshape(tok_rows * lax.axis_size("seq"), col_count)
        .astype(jnp.bfloat16),
        "seq",
        scatter_dimension=0,
        tiled=True,
    )
    feature_cols = normed
    value_curv = lax.psum_scatter(
        jnp.einsum(
            "tr,tc->rc", feature_cols, value_grad, preferred_element_type=jnp.float32
        ).astype(jnp.bfloat16),
        "seq",
        scatter_dimension=0,
        tiled=True,
    )
    return (value_curv, out_curv)


def solution(mesh):
    in_specs = (
        P(("groups", "seq"), None),
        P(("groups", "seq"), ("head", "rep")),
        P(("groups", "seq"), ("head", "rep")),
        P(("groups", "seq"), ("head", "rep")),
        P(("head", "rep"), "seq"),
        P(("groups", "seq"), ("head", "rep")),
        P(("groups", "head", "rep"), "seq"),
    )
    out_specs = (P(("groups", "seq"), ("head", "rep")), P(("groups", "head", "rep"), "seq"))
    return jax.shard_map(body, mesh=mesh, in_specs=in_specs, out_specs=out_specs, check_vma=False)
```

```python
from functools import partial

import jax
import jax.numpy as jnp
from jax import lax
from jax.experimental import pallas as pl
from jax.experimental.pallas import tpu as pltpu
from jax.sharding import PartitionSpec as P

DH = 64


VMEM = pl.BlockSpec(memory_space=pltpu.VMEM)
HBM = pl.BlockSpec(memory_space=pltpu.HBM)
ANY = pl.BlockSpec(memory_space=pl.ANY)


class Chain:
    def __init__(self):
        self.last = None

    def __call__(self, kernel, outs, ins, scratch=(), in_specs=None, first=()):
        specs = in_specs or [VMEM] * len(ins)
        out_specs = [HBM] * len(outs) if in_specs and HBM in in_specs and VMEM not in in_specs else [VMEM] * len(outs)
        count = len(ins)
        if self.last is not None:
            first = [*first, self.last]
        ins, specs = [*ins, *first], [*specs, *[ANY] * len(first)]

        def body(*refs):
            kernel(*refs[:count], *refs[len(ins) :])

        results = pl.pallas_call(
            body,
            out_shape=outs,
            in_specs=specs,
            out_specs=out_specs,
            scratch_shapes=list(scratch),
            compiler_params=pltpu.CompilerParams(vmem_limit_bytes=18 * 2**20),
            cost_estimate=pl.CostEstimate(flops=1, bytes_accessed=1, transcendentals=0),
            name=getattr(kernel, "func", kernel).__name__,
        )(*ins)
        self.last = results[0]
        return results


def bf(*shape):
    return jax.ShapeDtypeStruct(shape, jnp.bfloat16)


def dot(a, b, ca=1, cb=0):
    return lax.dot_general(a, b, (((ca,), (cb,)), ((), ())), preferred_element_type=jnp.float32)


def at(index, size):
    return pl.ds(pl.multiple_of(index * size, size), size)


def ahead(x, k):
    n = lax.axis_size("seq")
    return lax.ppermute(x, "seq", [(i, (i + k) % n) for i in range(n)])


def swap(x, axis):
    return lax.ppermute(x, axis, [(0, 1), (1, 0)])


def after(x, *first):
    return lax.optimization_barrier((x, *first))[0]


def pack(*refs):
    *pieces, weight, out, share, sem = refs
    copy = pltpu.make_async_copy(weight.at[at(lax.axis_index("groups"), share.shape[0])], share, sem)
    copy.start()
    for j, piece in enumerate(pieces):
        out[j] = piece[...]
    copy.wait()


def tangent_term(n, normed, packed, peer, probe, feats, *refs):
    outs, whole, sem = refs[:n], refs[n], refs[n + 1]
    me, head, rep = lax.axis_index("seq"), lax.axis_index("head"), lax.axis_index("rep")
    tok = normed.shape[0]
    part, slab = packed.shape[1:]
    copy = pltpu.make_async_copy(normed.at[:, at(me, slab)], feats.at[at(me, tok)], sem)
    copy.start()
    cols = outs[0].shape[1]
    for k in [*range(1, n), 0]:
        block = lax.rem(me - k + n, n)
        if k == 0:
            copy.wait()
        else:
            for rows, core in ((packed, rep), (peer, 1 - rep)):
                for row, side in ((k % (n - 1), head), (n - 1 + k % (n - 1), 1 - head)):
                    start = block * tok + (core * 2 + side) * part
                    feats[pl.ds(pl.multiple_of(start, part), part), :] = rows[row]
        whole[at(block, tok), :] = dot(feats[at(block, tok), :], probe[...]).astype(jnp.bfloat16)
    for k in range(n):
        outs[k][...] = whole[:, at(lax.rem(me + k, n), cols)]


def flip(feats, out):
    out[...] = feats[...].T


def keep_heads(parts):
    return jnp.concatenate([part[h * DH : (h + 1) * DH] for h, part in enumerate(parts)], axis=0)


def attend(n, *refs):
    own, pieces, (probs, attended, *all3) = refs[:3], refs[3 : n + 2], refs[n + 2 :]
    q_all, k_all, v_all = all3
    me = lax.axis_index("seq")
    tok, cols = pieces[0].shape[1:]
    for j in range(3):
        all3[j][at(me, tok), :] = own[j][:, at(me, cols)]
        for k in range(1, n):
            all3[j][at(lax.rem(me - k + n, n), tok), :] = pieces[k - 1][j]
    heads = cols // DH
    v_flip = v_all[...].T
    lane = lax.broadcasted_iota(jnp.int32, (tok, cols), 1) // DH

    @pl.loop(0, n)
    def _(c):
        rows = at(c, tok)
        parts = []
        for h in range(heads):
            query = jnp.where(lane == h, q_all[rows, :], 0)
            scores = dot(k_all[...], query, 1, 1)
            exps = jnp.exp(scores - jnp.max(scores, axis=0, keepdims=True))
            prob = (exps * (1.0 / jnp.sum(exps, axis=0, keepdims=True))).astype(jnp.bfloat16)
            probs[h, :, rows] = prob
            parts.append(dot(v_flip, prob))
        attended[rows, :] = keep_heads(parts).T.astype(jnp.bfloat16)


def halves(rows, home, away):
    head = lax.axis_index("head")
    half = home.shape[0]
    home[...] = rows[at(head, half), :]
    away[...] = rows[at(1 - head, half), :]


def attend_tan(n, *refs):
    terms, probs, (home, away, held, result, sems) = refs[:n], refs[n], refs[n + 1 :]
    heads = probs.shape[0]
    copies = [pltpu.make_async_copy(probs.at[h], held.at[h], sems.at[h]) for h in range(heads)]
    for copy in copies:
        copy.start()
    total = terms[0][...].astype(jnp.float32)
    for term in terms[1:]:
        total = total + term[...].astype(jnp.float32)
    flipped = total.T.astype(jnp.bfloat16)
    parts = []
    for h in range(heads):
        copies[h].wait()
        parts.append(dot(flipped, held[h]))
    result[...] = keep_heads(parts).T.astype(jnp.bfloat16)
    halves(result, home, away)


def add(one, two, out):
    out[...] = (one[...].astype(jnp.float32) + two[...].astype(jnp.float32)).astype(jnp.bfloat16)


def join(home, other, out):
    cols = home.shape[1]
    out[:, :cols] = home[...]
    out[:, cols:] = other[...]


def cut_rows(n, *refs):
    pieces, away = refs[:n], refs[n]
    me, head = lax.axis_index("seq"), lax.axis_index("head")
    half = away.shape[0]
    cols = pieces[0].shape[1]
    for k in range(n):
        away[:, at(lax.rem(me - k + n, n), cols)] = pieces[k][at(1 - head, half), :]


def out_term(n, *refs):
    pieces, (theirs, probe, other, total, lhs) = refs[:n], refs[n:]
    me, head = lax.axis_index("seq"), lax.axis_index("head")
    half = theirs.shape[0]
    cols = pieces[0].shape[1]
    for k in range(n):
        lhs[:, at(lax.rem(me - k + n, n), cols)] = pieces[k][at(head, half), :]
    total[...] = dot(lhs[...], probe[...])
    total[...] += dot(theirs[...], other[...])


def out_sum(n, *refs):
    base, pieces, (weight, one, two, out, lhs) = refs[0], refs[1 : n + 1], refs[n + 1 :]
    me, group = lax.axis_index("seq"), lax.axis_index("groups")
    cols = pieces[0].shape[1] // 2
    for k in range(n):
        where = at(lax.rem(me - k + n, n), cols)
        for d in range(2):
            lhs[d, :, where] = pieces[k][:, d * cols : (d + 1) * cols]
    rows = one.shape[0]
    total = base[...] + dot(lhs[0], weight[...])
    total = total + dot(lhs[1, :, at(group, rows)], one[...])
    out[...] = (total + dot(lhs[1, :, at(1 - group, rows)], two[...])).astype(jnp.bfloat16)


def grad_term(n, mine, other_core, weight, one, two, tangent_out, share, *refs):
    outs, grad = refs[:n], refs[n]
    me = lax.axis_index("seq")
    cols = outs[0].shape[1] // 2
    tangent_out[...] = (mine[...].astype(jnp.float32) + other_core[...].astype(jnp.float32)).astype(jnp.bfloat16)
    share[...] = tangent_out[at(lax.axis_index("rep"), share.shape[0]), :]
    group = lax.axis_index("groups")
    rows = one.shape[0]
    grad[0] = dot(tangent_out[...], weight[...], 1, 1).astype(jnp.bfloat16)
    grad[1, :, at(group, rows)] = dot(tangent_out[...], one[...], 1, 1).astype(jnp.bfloat16)
    grad[1, :, at(1 - group, rows)] = dot(tangent_out[...], two[...], 1, 1).astype(jnp.bfloat16)
    for d in range(2):
        for k in range(n):
            outs[k][:, d * cols : (d + 1) * cols] = grad[d, :, at(lax.rem(me + k, n), cols)]


def add_grad(n, *refs):
    terms, home, away = refs[:n], refs[n], refs[n + 1]
    total = terms[0][...].astype(jnp.float32)
    for term in terms[1:]:
        total = total + term[...].astype(jnp.float32)
    cols = home.shape[1]
    home[...] = total[:, :cols].astype(jnp.bfloat16)
    away[...] = total[:, cols:].astype(jnp.bfloat16)


def key_grad(mine, theirs, probs, out, grad, held, sems):
    heads, tokens, _ = probs.shape
    half, cols = mine.shape
    parts = held.shape[0]
    rows = tokens // parts
    copies = [pltpu.make_async_copy(probs.at[:, pl.ds(c * rows, rows)], held.at[c], sems.at[c]) for c in range(parts)]
    for copy in copies:
        copy.start()
    head = lax.axis_index("head")
    grad[at(head, half), :] = mine[...]
    grad[at(1 - head, half), :] = theirs[...]
    lane = lax.broadcasted_iota(jnp.int32, (rows, cols), 1) // DH
    for c in range(parts):
        copies[c].wait()
        value = dot(held[c, 0], grad[...])
        for h in range(1, heads):
            value = jnp.where(lane == h, dot(held[c, h], grad[...]), value)
        out[pl.ds(c * rows, rows), :] = value.astype(jnp.bfloat16)


def value_product(n, *refs):
    flipped, blocks, out, rhs = refs[0], refs[1 : n + 1], refs[n + 1], refs[n + 2]
    me = lax.axis_index("seq")
    cols = blocks[0].shape[1]
    for k in range(n):
        rhs[:, at(lax.rem(me - k + n, n), cols)] = blocks[k][...]
    out[...] = dot(flipped[...], rhs[...]).astype(jnp.bfloat16)


def out_product(n, *refs):
    pieces, (mine, one, two, out, rows) = refs[:n], refs[n:]
    me, head, rep = lax.axis_index("seq"), lax.axis_index("head"), lax.axis_index("rep")
    cols = pieces[0].shape[1]
    half, part = mine.shape[0], one.shape[0]
    rows[at(head, half), :] = mine[...]
    for index, piece in ((rep, one), (1 - rep, two)):
        start = (1 - head) * half + index * part
        rows[pl.ds(pl.multiple_of(start, part), part), :] = piece[...]
    for k in range(n):
        out[at(lax.rem(me - k + n, n), cols), :] = dot(pieces[k][...].T, rows[...]).astype(jnp.bfloat16)


def by_heads(normed, query_proj, key_proj, value_proj, out_weight, value_probe, out_probe):
    n = lax.axis_size("seq")
    me, head, rep = lax.axis_index("seq"), lax.axis_index("head"), lax.axis_index("rep")
    tok, width = normed.shape
    block = query_proj.shape[1]
    slab, cols, tokens = width // n, block // n, tok * n
    half, heads = tokens // 2, block // n // DH
    call = Chain()
    part = partial
    dma = pltpu.SemaphoreType.DMA
    f32 = jnp.float32

    def held(*shape):
        return pltpu.VMEM(shape, jnp.bfloat16)

    def gathered(x):
        pieces = [x] + [None] * (n - 1)
        for k in range(1, (n - 1) // 2 + 1):
            pieces[k] = ahead(pieces[k - 1], 1)
        for k in range(1, n // 2 + 1):
            pieces[n - k] = ahead(pieces[(n - k + 1) % n], n - 1)
        return pieces

    def summed(terms):
        sums = [terms[0]]
        for step, far in ((1, n // 2), (-1, (n - 1) // 2)):
            total = ahead(terms[step * far], step)
            for k in range(far - 1, 0, -1):
                (total,) = call(add, [bf(*total.shape)], [total, terms[step * k]])
                total = ahead(total, step)
            sums.append(total)
        return sums

    quarter = tok // 4
    start = (rep * 2 + head) * quarter
    got = [
        ahead(lax.dynamic_slice(normed, (start, lax.rem(me + k, n) * slab), (quarter, slab)), k) for k in range(1, n)]
    proj = (query_proj, key_proj, value_proj)
    qkv = []
    for k in range(1, n):
        piece = jnp.stack([lax.dynamic_slice(x, (0, lax.rem(me + k, n) * cols), (tok, cols)) for x in proj])
        qkv.append(ahead(after(piece, got[0]), k))
    got = got[-1:] + got[:-1]
    other = [swap(x, "head") for x in got]
    packed, share = call(
        pack, [bf(2 * (n - 1), quarter, slab), bf(block // 2, slab)], [*got, *other, out_weight],
        scratch=[dma(())], in_specs=[VMEM] * (2 * n - 2) + [ANY], first=qkv[:2])
    feats, *terms = call(
        part(tangent_term, n), [bf(tokens, slab)] + [bf(tokens, cols)] * n,
        [normed, packed, swap(packed, "rep"), value_probe], scratch=[held(tokens, block), dma(())],
        in_specs=[ANY] + [VMEM] * 3)
    other_probe = swap(after(out_probe, packed), "head")
    weights = [swap(after(share, feats), "head")]
    probs, attended = call(
        part(attend, n), [bf(heads, tokens, tokens), bf(tokens, cols)], [*proj, *qkv],
        scratch=[held(tokens, cols)] * 3)
    att = gathered(attended)
    tangent = summed(terms)
    tan, tan_away = call(
        part(attend_tan, 3), [bf(half, cols)] * 2, [*tangent, probs],
        scratch=[held(heads, tokens, tokens), held(tokens, cols), dma((heads,))], in_specs=[VMEM] * 3 + [ANY])
    (tan,) = call(join, [bf(half, 2 * cols)], [tan, swap(tan_away, "head")], first=[att[1], att[-1]])
    weights.append(swap(weights[0], "groups"))
    tan = gathered(tan)
    (away,) = call(part(cut_rows, n), [bf(half, block)], att)
    (base,) = call(
        part(out_term, n), [jax.ShapeDtypeStruct((half, slab), f32)],
        [*att, swap(away, "head"), out_probe, other_probe], scratch=[held(half, block)])
    (mine,) = call(
        part(out_sum, n), [bf(half, slab)], [base, *tan, out_weight, *weights], scratch=[held(2, half, block)])
    tangent_out, share, *grads = call(
        part(grad_term, n), [bf(half, slab), bf(half // 2, slab)] + [bf(half, 2 * cols)] * n,
        [mine, swap(mine, "rep"), out_weight, *weights],
        scratch=[held(2, half, block)])
    home, away = call(part(add_grad, 3), [bf(half, cols)] * 2, summed(grads))
    (value_grad,) = call(
        key_grad, [bf(tokens, cols)], [home, swap(away, "head"), probs],
        scratch=[held(tokens, cols), held(4, heads, tokens // 4, tokens), dma((4,))], in_specs=[VMEM] * 2 + [ANY])
    value_grad = gathered(value_grad)
    share = swap(share, "head")
    (out_curv,) = call(
        part(out_product, n), [bf(block, slab)], [*att, tangent_out, share, swap(share, "rep")],
        scratch=[held(tokens, slab)])
    (flipped,) = call(flip, [bf(slab, tokens)], [feats])
    (value_curv,) = call(
        part(value_product, n), [bf(slab, block)], [flipped, *value_grad], scratch=[held(tokens, block)])
    return value_curv, out_curv


def body(*args):
    tok, cols = args[1].shape
    n = lax.axis_size("seq")
    even = cols % (n * 128) == 0 and tok % 64 == 0 and tok * n % 64 == 0
    if even and all(lax.axis_size(axis) == 2 for axis in ("groups", "head", "rep")):
        return by_heads(*args)
    return by_tokens(*args)


def by_tokens(normed, query_proj, key_proj, value_proj, out_weight, value_probe, out_probe):
    tok_rows = normed.shape[0]
    col_count = query_proj.shape[1]
    local_heads = col_count // DH
    feature_cols = normed
    value_tangent = jnp.dot(
        feature_cols,
        lax.all_gather(value_probe, "seq", axis=0, tiled=True),
        preferred_element_type=jnp.float32,
    ).astype(jnp.bfloat16)
    query_heads = query_proj.reshape(tok_rows, local_heads, DH)
    run_max = jnp.full((tok_rows, local_heads), -1e30, jnp.float32)
    key_rows = lax.all_gather(key_proj, "seq", axis=0, tiled=True)
    value_rows = lax.all_gather(value_proj, "seq", axis=0, tiled=True)
    tangent_rows = lax.all_gather(value_tangent, "seq", axis=0, tiled=True)
    piece_rows = key_rows.shape[0]
    key_heads = key_rows.reshape(piece_rows, local_heads, DH)
    value_heads = value_rows.reshape(piece_rows, local_heads, DH)
    tangent_heads = tangent_rows.reshape(piece_rows, local_heads, DH)
    scores = jnp.einsum("qhd,khd->qhk", query_heads, key_heads, preferred_element_type=jnp.float32)
    next_max = jnp.maximum(run_max, jnp.max(scores, axis=2))
    exp_rows = jnp.exp(scores - next_max[:, :, None])
    run_sum = jnp.sum(exp_rows, axis=2)
    prob_bf = exp_rows.astype(jnp.bfloat16)
    accum_v = jnp.einsum("qhk,khd->qhd", prob_bf, value_heads, preferred_element_type=jnp.float32)
    accum_t = jnp.einsum("qhk,khd->qhd", prob_bf, tangent_heads, preferred_element_type=jnp.float32)
    run_max, run_sum, accum_v, accum_t = (next_max, run_sum, accum_v, accum_t)
    row_lse = run_max + jnp.log(run_sum)
    attended = (accum_v / run_sum[:, :, None]).reshape(tok_rows, col_count).astype(jnp.bfloat16)
    attended_tan = (accum_t / run_sum[:, :, None]).reshape(tok_rows, col_count).astype(jnp.bfloat16)
    weight_full, probe_full = (
        lax.all_gather(out_weight, "seq", axis=1, tiled=True),
        lax.all_gather(out_probe, "seq", axis=1, tiled=True),
    )
    partial_out = jnp.dot(attended_tan, weight_full, preferred_element_type=jnp.float32) + jnp.dot(
        attended, probe_full, preferred_element_type=jnp.float32
    )
    tangent_out = lax.psum(partial_out.astype(jnp.bfloat16), ("head", "rep"))
    out_term = jnp.einsum("tc,td->cd", attended, tangent_out, preferred_element_type=jnp.float32)
    out_curv = lax.psum_scatter(
        out_term.astype(jnp.bfloat16), "seq", scatter_dimension=1, tiled=True
    )
    grad_out = jnp.einsum(
        "td,cd->tc", tangent_out, weight_full, preferred_element_type=jnp.float32
    ).astype(jnp.bfloat16)
    grad_heads = grad_out.reshape(tok_rows, local_heads, DH)
    every_key = lax.all_gather(key_proj, "seq", axis=0, tiled=True)
    key_rows = every_key.reshape(tok_rows * lax.axis_size("seq"), local_heads, DH)
    scores = jnp.einsum("qhd,khd->qhk", query_heads, key_rows, preferred_element_type=jnp.float32)
    prob_bf = jnp.exp(scores - row_lse[:, :, None]).astype(jnp.bfloat16)
    value_grad = lax.psum_scatter(
        jnp.einsum("qhk,qhd->khd", prob_bf, grad_heads, preferred_element_type=jnp.float32)
        .reshape(tok_rows * lax.axis_size("seq"), col_count)
        .astype(jnp.bfloat16),
        "seq",
        scatter_dimension=0,
        tiled=True,
    )
    feature_cols = normed
    value_curv = lax.psum_scatter(
        jnp.einsum(
            "tr,tc->rc", feature_cols, value_grad, preferred_element_type=jnp.float32
        ).astype(jnp.bfloat16),
        "seq",
        scatter_dimension=0,
        tiled=True,
    )
    return (value_curv, out_curv)


def solution(mesh):
    in_specs = (
        P(("groups", "seq"), None),
        P(("groups", "seq"), ("head", "rep")),
        P(("groups", "seq"), ("head", "rep")),
        P(("groups", "seq"), ("head", "rep")),
        P(("head", "rep"), "seq"),
        P(("groups", "seq"), ("head", "rep")),
        P(("groups", "head", "rep"), "seq"),
    )
    out_specs = (P(("groups", "seq"), ("head", "rep")), P(("groups", "head", "rep"), "seq"))
    return jax.shard_map(body, mesh=mesh, in_specs=in_specs, out_specs=out_specs, check_vma=False)
```

```python
from functools import partial

import jax
import jax.numpy as jnp
from jax import lax
from jax.experimental import pallas as pl
from jax.experimental.pallas import tpu as pltpu
from jax.sharding import PartitionSpec as P

DH = 64


VMEM = pl.BlockSpec(memory_space=pltpu.VMEM)
HBM = pl.BlockSpec(memory_space=pltpu.HBM)
ANY = pl.BlockSpec(memory_space=pl.ANY)


class Chain:
    def __init__(self):
        self.last = None

    def __call__(self, kernel, outs, ins, scratch=(), in_specs=None, first=()):
        specs = in_specs or [VMEM] * len(ins)
        out_specs = [HBM] * len(outs) if in_specs and HBM in in_specs and VMEM not in in_specs else [VMEM] * len(outs)
        count = len(ins)
        if self.last is not None:
            first = [*first, self.last]
        ins, specs = [*ins, *first], [*specs, *[ANY] * len(first)]

        def body(*refs):
            kernel(*refs[:count], *refs[len(ins) :])

        results = pl.pallas_call(
            body,
            out_shape=outs,
            in_specs=specs,
            out_specs=out_specs,
            scratch_shapes=list(scratch),
            compiler_params=pltpu.CompilerParams(vmem_limit_bytes=18 * 2**20),
            cost_estimate=pl.CostEstimate(flops=1, bytes_accessed=1, transcendentals=0),
            name=getattr(kernel, "func", kernel).__name__,
        )(*ins)
        self.last = results[0]
        return results


def bf(*shape):
    return jax.ShapeDtypeStruct(shape, jnp.bfloat16)


def dot(a, b, ca=1, cb=0):
    return lax.dot_general(a, b, (((ca,), (cb,)), ((), ())), preferred_element_type=jnp.float32)


def at(index, size):
    return pl.ds(pl.multiple_of(index * size, size), size)


def ahead(x, k):
    n = lax.axis_size("seq")
    return lax.ppermute(x, "seq", [(i, (i + k) % n) for i in range(n)])


def swap(x, axis):
    return lax.ppermute(x, axis, [(0, 1), (1, 0)])


def after(x, *first):
    return lax.optimization_barrier((x, *first))[0]


def pack(*refs):
    *pieces, weight, out, share, sem = refs
    copy = pltpu.make_async_copy(weight.at[at(lax.axis_index("groups"), share.shape[0])], share, sem)
    copy.start()
    for j, piece in enumerate(pieces):
        out[j] = piece[...]
    copy.wait()


def tangent_term(n, normed, packed, peer, probe, feats, *refs):
    outs, whole, sem = refs[:n], refs[n], refs[n + 1]
    me, head, rep = lax.axis_index("seq"), lax.axis_index("head"), lax.axis_index("rep")
    tok = normed.shape[0]
    part, slab = packed.shape[1:]
    copy = pltpu.make_async_copy(normed.at[:, at(me, slab)], feats.at[at(me, tok)], sem)
    copy.start()
    cols = outs[0].shape[1]
    for k in [*range(1, n), 0]:
        block = lax.rem(me - k + n, n)
        if k == 0:
            copy.wait()
        else:
            for rows, core in ((packed, rep), (peer, 1 - rep)):
                for row, side in ((k % (n - 1), head), (n - 1 + k % (n - 1), 1 - head)):
                    start = block * tok + (core * 2 + side) * part
                    feats[pl.ds(pl.multiple_of(start, part), part), :] = rows[row]
        whole[at(block, tok), :] = dot(feats[at(block, tok), :], probe[...]).astype(jnp.bfloat16)
    for k in range(n):
        outs[k][...] = whole[:, at(lax.rem(me + k, n), cols)]


def flip(feats, out):
    out[...] = feats[...].T


def keep_heads(parts):
    return jnp.concatenate([part[h * DH : (h + 1) * DH] for h, part in enumerate(parts)], axis=0)


def attend(n, *refs):
    own, pieces, (probs, attended, *all3) = refs[:3], refs[3 : n + 2], refs[n + 2 :]
    q_all, k_all, v_all = all3
    me = lax.axis_index("seq")
    tok, cols = pieces[0].shape[1:]
    for j in range(3):
        all3[j][at(me, tok), :] = own[j][:, at(me, cols)]
        for k in range(1, n):
            all3[j][at(lax.rem(me - k + n, n), tok), :] = pieces[k - 1][j]
    heads = cols // DH
    v_flip = v_all[...].T
    lane = lax.broadcasted_iota(jnp.int32, (tok, cols), 1) // DH

    @pl.loop(0, n)
    def _(c):
        rows = at(c, tok)
        parts = []
        for h in range(heads):
            query = jnp.where(lane == h, q_all[rows, :], 0)
            scores = dot(k_all[...], query, 1, 1)
            exps = jnp.exp(scores - jnp.max(scores, axis=0, keepdims=True))
            prob = (exps * (1.0 / jnp.sum(exps, axis=0, keepdims=True))).astype(jnp.bfloat16)
            probs[h, :, rows] = prob
            parts.append(dot(v_flip, prob))
        attended[rows, :] = keep_heads(parts).T.astype(jnp.bfloat16)


def halves(rows, home, away):
    head = lax.axis_index("head")
    half = home.shape[0]
    home[...] = rows[at(head, half), :]
    away[...] = rows[at(1 - head, half), :]


def attend_tan(n, *refs):
    terms, probs, (home, away, held, result, sems) = refs[:n], refs[n], refs[n + 1 :]
    heads = probs.shape[0]
    copies = [pltpu.make_async_copy(probs.at[h], held.at[h], sems.at[h]) for h in range(heads)]
    for copy in copies:
        copy.start()
    total = terms[0][...].astype(jnp.float32)
    for term in terms[1:]:
        total = total + term[...].astype(jnp.float32)
    flipped = total.T.astype(jnp.bfloat16)
    parts = []
    for h in range(heads):
        copies[h].wait()
        parts.append(dot(flipped, held[h]))
    result[...] = keep_heads(parts).T.astype(jnp.bfloat16)
    halves(result, home, away)


def add(one, two, out):
    out[...] = (one[...].astype(jnp.float32) + two[...].astype(jnp.float32)).astype(jnp.bfloat16)


def join(home, other, out):
    cols = home.shape[1]
    out[:, :cols] = home[...]
    out[:, cols:] = other[...]


def cut_rows(n, *refs):
    pieces, away = refs[:n], refs[n]
    me, head = lax.axis_index("seq"), lax.axis_index("head")
    half = away.shape[0]
    cols = pieces[0].shape[1]
    for k in range(n):
        away[:, at(lax.rem(me - k + n, n), cols)] = pieces[k][at(1 - head, half), :]


def out_term(n, *refs):
    pieces, (theirs, probe, other, total, lhs) = refs[:n], refs[n:]
    me, head = lax.axis_index("seq"), lax.axis_index("head")
    half = theirs.shape[0]
    cols = pieces[0].shape[1]
    for k in range(n):
        lhs[:, at(lax.rem(me - k + n, n), cols)] = pieces[k][at(head, half), :]
    total[...] = dot(lhs[...], probe[...])
    total[...] += dot(theirs[...], other[...])


def out_sum(n, *refs):
    base, pieces, (weight, one, two, out, lhs) = refs[0], refs[1 : n + 1], refs[n + 1 :]
    me, group = lax.axis_index("seq"), lax.axis_index("groups")
    cols = pieces[0].shape[1] // 2
    for k in range(n):
        where = at(lax.rem(me - k + n, n), cols)
        for d in range(2):
            lhs[d, :, where] = pieces[k][:, d * cols : (d + 1) * cols]
    rows = one.shape[0]
    total = base[...] + dot(lhs[0], weight[...])
    total = total + dot(lhs[1, :, at(group, rows)], one[...])
    out[...] = (total + dot(lhs[1, :, at(1 - group, rows)], two[...])).astype(jnp.bfloat16)


def grad_far(n, mine, other_core, weight, one, two, tangent_out, share, out):
    me, group = lax.axis_index("seq"), lax.axis_index("groups")
    cols = out.shape[1] // 2
    tangent_out[...] = (mine[...].astype(jnp.float32) + other_core[...].astype(jnp.float32)).astype(jnp.bfloat16)
    share[...] = tangent_out[at(lax.axis_index("rep"), share.shape[0]), :]
    where = lax.rem(me + n // 2, n)
    out[:, :cols] = dot(tangent_out[...], weight[at(where, cols), :], 1, 1).astype(jnp.bfloat16)
    near = where // (n // 2) == group

    @pl.when(near)
    def _():
        rows = one[at(lax.rem(where, n // 2), cols), :]
        out[:, cols:] = dot(tangent_out[...], rows, 1, 1).astype(jnp.bfloat16)

    @pl.when(jnp.logical_not(near))
    def _():
        rows = two[at(lax.rem(where, n // 2), cols), :]
        out[:, cols:] = dot(tangent_out[...], rows, 1, 1).astype(jnp.bfloat16)


def grad_term(n, tangent_out, weight, one, two, *refs):
    outs, grad = refs[: n - 1], refs[n - 1]
    me, group = lax.axis_index("seq"), lax.axis_index("groups")
    cols = outs[0].shape[1] // 2
    rows = one.shape[0]
    grad[0] = dot(tangent_out[...], weight[...], 1, 1).astype(jnp.bfloat16)
    grad[1, :, at(group, rows)] = dot(tangent_out[...], one[...], 1, 1).astype(jnp.bfloat16)
    grad[1, :, at(1 - group, rows)] = dot(tangent_out[...], two[...], 1, 1).astype(jnp.bfloat16)
    for d in range(2):
        for j, k in enumerate(k for k in range(n) if k != n // 2):
            outs[j][:, d * cols : (d + 1) * cols] = grad[d, :, at(lax.rem(me + k, n), cols)]


def add_grad(n, *refs):
    terms, home, away = refs[:n], refs[n], refs[n + 1]
    total = terms[0][...].astype(jnp.float32)
    for term in terms[1:]:
        total = total + term[...].astype(jnp.float32)
    cols = home.shape[1]
    home[...] = total[:, :cols].astype(jnp.bfloat16)
    away[...] = total[:, cols:].astype(jnp.bfloat16)


def key_grad(mine, theirs, probs, out, grad, held, sems):
    heads, tokens, _ = probs.shape
    half, cols = mine.shape
    parts = held.shape[0]
    rows = tokens // parts
    copies = [pltpu.make_async_copy(probs.at[:, pl.ds(c * rows, rows)], held.at[c], sems.at[c]) for c in range(parts)]
    for copy in copies:
        copy.start()
    head = lax.axis_index("head")
    grad[at(head, half), :] = mine[...]
    grad[at(1 - head, half), :] = theirs[...]
    lane = lax.broadcasted_iota(jnp.int32, (rows, cols), 1) // DH
    for c in range(parts):
        copies[c].wait()
        value = dot(held[c, 0], grad[...])
        for h in range(1, heads):
            value = jnp.where(lane == h, dot(held[c, h], grad[...]), value)
        out[pl.ds(c * rows, rows), :] = value.astype(jnp.bfloat16)


def value_product(n, *refs):
    flipped, blocks, out, rhs = refs[0], refs[1 : n + 1], refs[n + 1], refs[n + 2]
    me = lax.axis_index("seq")
    cols = blocks[0].shape[1]
    for k in range(n):
        rhs[:, at(lax.rem(me - k + n, n), cols)] = blocks[k][...]
    out[...] = dot(flipped[...], rhs[...]).astype(jnp.bfloat16)


def out_product(n, *refs):
    pieces, (mine, one, two, out, rows) = refs[:n], refs[n:]
    me, head, rep = lax.axis_index("seq"), lax.axis_index("head"), lax.axis_index("rep")
    cols = pieces[0].shape[1]
    half, part = mine.shape[0], one.shape[0]
    rows[at(head, half), :] = mine[...]
    for index, piece in ((rep, one), (1 - rep, two)):
        start = (1 - head) * half + index * part
        rows[pl.ds(pl.multiple_of(start, part), part), :] = piece[...]
    for k in range(n):
        out[at(lax.rem(me - k + n, n), cols), :] = dot(pieces[k][...].T, rows[...]).astype(jnp.bfloat16)


def by_heads(normed, query_proj, key_proj, value_proj, out_weight, value_probe, out_probe):
    n = lax.axis_size("seq")
    me, head, rep = lax.axis_index("seq"), lax.axis_index("head"), lax.axis_index("rep")
    tok, width = normed.shape
    block = query_proj.shape[1]
    slab, cols, tokens = width // n, block // n, tok * n
    half, heads = tokens // 2, block // n // DH
    call = Chain()
    part = partial
    dma = pltpu.SemaphoreType.DMA
    f32 = jnp.float32

    def held(*shape):
        return pltpu.VMEM(shape, jnp.bfloat16)

    def gathered(x):
        pieces = [x] + [None] * (n - 1)
        for k in range(1, (n - 1) // 2 + 1):
            pieces[k] = ahead(pieces[k - 1], 1)
        for k in range(1, n // 2 + 1):
            pieces[n - k] = ahead(pieces[(n - k + 1) % n], n - 1)
        return pieces

    def summed(terms):
        sums = [terms[0]]
        for step, far in ((1, n // 2), (-1, (n - 1) // 2)):
            total = ahead(terms[step * far], step)
            for k in range(far - 1, 0, -1):
                (total,) = call(add, [bf(*total.shape)], [total, terms[step * k]])
                total = ahead(total, step)
            sums.append(total)
        return sums

    quarter = tok // 4
    start = (rep * 2 + head) * quarter
    got = [
        ahead(lax.dynamic_slice(normed, (start, lax.rem(me + k, n) * slab), (quarter, slab)), k) for k in range(1, n)]
    proj = (query_proj, key_proj, value_proj)
    qkv = []
    for k in range(1, n):
        piece = jnp.stack([lax.dynamic_slice(x, (0, lax.rem(me + k, n) * cols), (tok, cols)) for x in proj])
        qkv.append(ahead(after(piece, got[0]), k))
    got = got[-1:] + got[:-1]
    other = [swap(x, "head") for x in got]
    packed, share = call(
        pack, [bf(2 * (n - 1), quarter, slab), bf(block // 2, slab)], [*got, *other, out_weight],
        scratch=[dma(())], in_specs=[VMEM] * (2 * n - 2) + [ANY], first=qkv[:2])
    feats, *terms = call(
        part(tangent_term, n), [bf(tokens, slab)] + [bf(tokens, cols)] * n,
        [normed, packed, swap(packed, "rep"), value_probe], scratch=[held(tokens, block), dma(())],
        in_specs=[ANY] + [VMEM] * 3)
    other_probe = swap(after(out_probe, packed), "head")
    weights = [swap(after(share, feats), "head")]
    probs, attended = call(
        part(attend, n), [bf(heads, tokens, tokens), bf(tokens, cols)], [*proj, *qkv],
        scratch=[held(tokens, cols)] * 3)
    att = gathered(attended)
    tangent = summed(terms)
    tan, tan_away = call(
        part(attend_tan, 3), [bf(half, cols)] * 2, [*tangent, probs],
        scratch=[held(heads, tokens, tokens), held(tokens, cols), dma((heads,))], in_specs=[VMEM] * 3 + [ANY])
    (tan,) = call(join, [bf(half, 2 * cols)], [tan, swap(tan_away, "head")], first=[att[1], att[-1]])
    weights.append(swap(weights[0], "groups"))
    tan = gathered(tan)
    (away,) = call(part(cut_rows, n), [bf(half, block)], att)
    (base,) = call(
        part(out_term, n), [jax.ShapeDtypeStruct((half, slab), f32)],
        [*att, swap(away, "head"), out_probe, other_probe], scratch=[held(half, block)])
    (mine,) = call(
        part(out_sum, n), [bf(half, slab)], [base, *tan, out_weight, *weights], scratch=[held(2, half, block)])
    tangent_out, share, far = call(
        part(grad_far, n), [bf(half, slab), bf(half // 2, slab), bf(half, 2 * cols)],
        [mine, swap(mine, "rep"), out_weight, *weights])
    grads = call(
        part(grad_term, n), [bf(half, 2 * cols)] * (n - 1), [tangent_out, out_weight, *weights],
        scratch=[held(2, half, block)])
    grads = [*grads[: n // 2], far, *grads[n // 2 :]]
    home, away = call(part(add_grad, 3), [bf(half, cols)] * 2, summed(grads))
    (value_grad,) = call(
        key_grad, [bf(tokens, cols)], [home, swap(away, "head"), probs],
        scratch=[held(tokens, cols), held(4, heads, tokens // 4, tokens), dma((4,))], in_specs=[VMEM] * 2 + [ANY])
    value_grad = gathered(value_grad)
    share = swap(share, "head")
    (out_curv,) = call(
        part(out_product, n), [bf(block, slab)], [*att, tangent_out, share, swap(share, "rep")],
        scratch=[held(tokens, slab)])
    (flipped,) = call(flip, [bf(slab, tokens)], [feats])
    (value_curv,) = call(
        part(value_product, n), [bf(slab, block)], [flipped, *value_grad], scratch=[held(tokens, block)])
    return value_curv, out_curv


def body(*args):
    tok, cols = args[1].shape
    n = lax.axis_size("seq")
    even = n % 2 == 0 and cols % (n * 128) == 0 and tok % 64 == 0 and tok * n % 64 == 0
    if even and all(lax.axis_size(axis) == 2 for axis in ("groups", "head", "rep")):
        return by_heads(*args)
    return by_tokens(*args)


def by_tokens(normed, query_proj, key_proj, value_proj, out_weight, value_probe, out_probe):
    tok_rows = normed.shape[0]
    col_count = query_proj.shape[1]
    local_heads = col_count // DH
    feature_cols = normed
    value_tangent = jnp.dot(
        feature_cols,
        lax.all_gather(value_probe, "seq", axis=0, tiled=True),
        preferred_element_type=jnp.float32,
    ).astype(jnp.bfloat16)
    query_heads = query_proj.reshape(tok_rows, local_heads, DH)
    run_max = jnp.full((tok_rows, local_heads), -1e30, jnp.float32)
    key_rows = lax.all_gather(key_proj, "seq", axis=0, tiled=True)
    value_rows = lax.all_gather(value_proj, "seq", axis=0, tiled=True)
    tangent_rows = lax.all_gather(value_tangent, "seq", axis=0, tiled=True)
    piece_rows = key_rows.shape[0]
    key_heads = key_rows.reshape(piece_rows, local_heads, DH)
    value_heads = value_rows.reshape(piece_rows, local_heads, DH)
    tangent_heads = tangent_rows.reshape(piece_rows, local_heads, DH)
    scores = jnp.einsum("qhd,khd->qhk", query_heads, key_heads, preferred_element_type=jnp.float32)
    next_max = jnp.maximum(run_max, jnp.max(scores, axis=2))
    exp_rows = jnp.exp(scores - next_max[:, :, None])
    run_sum = jnp.sum(exp_rows, axis=2)
    prob_bf = exp_rows.astype(jnp.bfloat16)
    accum_v = jnp.einsum("qhk,khd->qhd", prob_bf, value_heads, preferred_element_type=jnp.float32)
    accum_t = jnp.einsum("qhk,khd->qhd", prob_bf, tangent_heads, preferred_element_type=jnp.float32)
    run_max, run_sum, accum_v, accum_t = (next_max, run_sum, accum_v, accum_t)
    row_lse = run_max + jnp.log(run_sum)
    attended = (accum_v / run_sum[:, :, None]).reshape(tok_rows, col_count).astype(jnp.bfloat16)
    attended_tan = (accum_t / run_sum[:, :, None]).reshape(tok_rows, col_count).astype(jnp.bfloat16)
    weight_full, probe_full = (
        lax.all_gather(out_weight, "seq", axis=1, tiled=True),
        lax.all_gather(out_probe, "seq", axis=1, tiled=True),
    )
    partial_out = jnp.dot(attended_tan, weight_full, preferred_element_type=jnp.float32) + jnp.dot(
        attended, probe_full, preferred_element_type=jnp.float32
    )
    tangent_out = lax.psum(partial_out.astype(jnp.bfloat16), ("head", "rep"))
    out_term = jnp.einsum("tc,td->cd", attended, tangent_out, preferred_element_type=jnp.float32)
    out_curv = lax.psum_scatter(
        out_term.astype(jnp.bfloat16), "seq", scatter_dimension=1, tiled=True
    )
    grad_out = jnp.einsum(
        "td,cd->tc", tangent_out, weight_full, preferred_element_type=jnp.float32
    ).astype(jnp.bfloat16)
    grad_heads = grad_out.reshape(tok_rows, local_heads, DH)
    every_key = lax.all_gather(key_proj, "seq", axis=0, tiled=True)
    key_rows = every_key.reshape(tok_rows * lax.axis_size("seq"), local_heads, DH)
    scores = jnp.einsum("qhd,khd->qhk", query_heads, key_rows, preferred_element_type=jnp.float32)
    prob_bf = jnp.exp(scores - row_lse[:, :, None]).astype(jnp.bfloat16)
    value_grad = lax.psum_scatter(
        jnp.einsum("qhk,qhd->khd", prob_bf, grad_heads, preferred_element_type=jnp.float32)
        .reshape(tok_rows * lax.axis_size("seq"), col_count)
        .astype(jnp.bfloat16),
        "seq",
        scatter_dimension=0,
        tiled=True,
    )
    feature_cols = normed
    value_curv = lax.psum_scatter(
        jnp.einsum(
            "tr,tc->rc", feature_cols, value_grad, preferred_element_type=jnp.float32
        ).astype(jnp.bfloat16),
        "seq",
        scatter_dimension=0,
        tiled=True,
    )
    return (value_curv, out_curv)


def solution(mesh):
    in_specs = (
        P(("groups", "seq"), None),
        P(("groups", "seq"), ("head", "rep")),
        P(("groups", "seq"), ("head", "rep")),
        P(("groups", "seq"), ("head", "rep")),
        P(("head", "rep"), "seq"),
        P(("groups", "seq"), ("head", "rep")),
        P(("groups", "head", "rep"), "seq"),
    )
    out_specs = (P(("groups", "seq"), ("head", "rep")), P(("groups", "head", "rep"), "seq"))
    return jax.shard_map(body, mesh=mesh, in_specs=in_specs, out_specs=out_specs, check_vma=False)
```

```python
from functools import partial

import jax
import jax.numpy as jnp
from jax import lax
from jax.experimental import pallas as pl
from jax.experimental.pallas import tpu as pltpu
from jax.sharding import PartitionSpec as P

DH = 64


VMEM = pl.BlockSpec(memory_space=pltpu.VMEM)
HBM = pl.BlockSpec(memory_space=pltpu.HBM)
ANY = pl.BlockSpec(memory_space=pl.ANY)


class Chain:
    def __init__(self):
        self.last = None

    def __call__(self, kernel, outs, ins, scratch=(), in_specs=None, first=(), mib=18):
        specs = in_specs or [VMEM] * len(ins)
        out_specs = [HBM] * len(outs) if in_specs and HBM in in_specs and VMEM not in in_specs else [VMEM] * len(outs)
        count = len(ins)
        if self.last is not None:
            first = [*first, self.last]
        ins, specs = [*ins, *first], [*specs, *[ANY] * len(first)]

        def body(*refs):
            kernel(*refs[:count], *refs[len(ins) :])

        results = pl.pallas_call(
            body,
            out_shape=outs,
            in_specs=specs,
            out_specs=out_specs,
            scratch_shapes=list(scratch),
            compiler_params=pltpu.CompilerParams(vmem_limit_bytes=mib * 2**20),
            cost_estimate=pl.CostEstimate(flops=1, bytes_accessed=1, transcendentals=0),
            name=getattr(kernel, "func", kernel).__name__,
        )(*ins)
        self.last = results[0]
        return results


def bf(*shape):
    return jax.ShapeDtypeStruct(shape, jnp.bfloat16)


def dot(a, b, ca=1, cb=0):
    return lax.dot_general(a, b, (((ca,), (cb,)), ((), ())), preferred_element_type=jnp.float32)


def at(index, size):
    return pl.ds(pl.multiple_of(index * size, size), size)


def ahead(x, k):
    n = lax.axis_size("seq")
    return lax.ppermute(x, "seq", [(i, (i + k) % n) for i in range(n)])


def swap(x, axis):
    return lax.ppermute(x, axis, [(0, 1), (1, 0)])


def after(x, *first):
    return lax.optimization_barrier((x, *first))[0]


def pack(*refs):
    *pieces, weight, probe, out, share, upper, lower, sems = refs
    rows = share.shape[0]
    copies = [
        pltpu.make_async_copy(weight.at[at(lax.axis_index("groups"), rows)], share, sems.at[0]),
        pltpu.make_async_copy(probe.at[pl.ds(0, rows)], upper, sems.at[1]),
        pltpu.make_async_copy(probe.at[pl.ds(rows, rows)], lower, sems.at[2]),
    ]
    for copy in copies:
        copy.start()
    for j, piece in enumerate(pieces):
        out[j] = piece[...]
    for copy in copies:
        copy.wait()


def tangent_term(n, normed, packed, peer, probe, feats, *refs):
    outs, whole, sem = refs[:n], refs[n], refs[n + 1]
    me, head, rep = lax.axis_index("seq"), lax.axis_index("head"), lax.axis_index("rep")
    tok = normed.shape[0]
    part, slab = packed.shape[1:]
    copy = pltpu.make_async_copy(normed.at[:, at(me, slab)], feats.at[at(me, tok)], sem)
    copy.start()
    cols = outs[0].shape[1]
    for k in [*range(1, n), 0]:
        block = lax.rem(me - k + n, n)
        if k == 0:
            copy.wait()
        else:
            for rows, core in ((packed, rep), (peer, 1 - rep)):
                for row, side in ((k % (n - 1), head), (n - 1 + k % (n - 1), 1 - head)):
                    start = block * tok + (core * 2 + side) * part
                    feats[pl.ds(pl.multiple_of(start, part), part), :] = rows[row]
        whole[at(block, tok), :] = dot(feats[at(block, tok), :], probe[...]).astype(jnp.bfloat16)
    for k in range(n):
        outs[k][...] = whole[:, at(lax.rem(me + k, n), cols)]


def flip(feats, out):
    out[...] = feats[...].T


def keep_heads(parts):
    return jnp.concatenate([part[h * DH : (h + 1) * DH] for h, part in enumerate(parts)], axis=0)


def attend(n, *refs):
    own, pieces, (probs, attended, *all3) = refs[:3], refs[3 : n + 2], refs[n + 2 :]
    q_all, k_all, v_all = all3
    me = lax.axis_index("seq")
    tok, cols = pieces[0].shape[1:]
    for j in range(3):
        all3[j][at(me, tok), :] = own[j][:, at(me, cols)]
        for k in range(1, n):
            all3[j][at(lax.rem(me - k + n, n), tok), :] = pieces[k - 1][j]
    heads = cols // DH
    v_flip = v_all[...].T
    step = probs.shape[2] // 2
    lane = lax.broadcasted_iota(jnp.int32, (step, cols), 1) // DH
    for c in range(2):
        rows = slice(c * step, (c + 1) * step)
        scores = [dot(k_all[...], jnp.where(lane == h, q_all[rows, :], 0), 1, 1) for h in range(heads)]
        parts = []
        for h in range(heads):
            exps = jnp.exp(scores[h] - jnp.max(scores[h], axis=0, keepdims=True))
            prob = (exps * (1.0 / jnp.sum(exps, axis=0, keepdims=True))).astype(jnp.bfloat16)
            probs[h, :, rows] = prob
            parts.append(dot(v_flip, prob))
        attended[rows, :] = keep_heads(parts).T.astype(jnp.bfloat16)


def halves(rows, home, away):
    head = lax.axis_index("head")
    half = home.shape[0]
    home[...] = rows[at(head, half), :]
    away[...] = rows[at(1 - head, half), :]


def attend_tan(n, *refs):
    terms, probs, (home, away, held, result, sems) = refs[:n], refs[n], refs[n + 1 :]
    heads = probs.shape[0]
    copies = [pltpu.make_async_copy(probs.at[h], held.at[h], sems.at[h]) for h in range(heads)]
    for copy in copies:
        copy.start()
    total = terms[0][...].astype(jnp.float32)
    for term in terms[1:]:
        total = total + term[...].astype(jnp.float32)
    flipped = total.T.astype(jnp.bfloat16)
    parts = []
    for h in range(heads):
        copies[h].wait()
        parts.append(dot(flipped, held[h]))
    result[...] = keep_heads(parts).T.astype(jnp.bfloat16)
    halves(result, home, away)


def add(one, two, out):
    out[...] = (one[...].astype(jnp.float32) + two[...].astype(jnp.float32)).astype(jnp.bfloat16)


def join(home, other, out):
    cols = home.shape[1]
    out[:, :cols] = home[...]
    out[:, cols:] = other[...]


def cut_rows(n, *refs):
    pieces, away = refs[:n], refs[n]
    me, head = lax.axis_index("seq"), lax.axis_index("head")
    half = away.shape[0]
    cols = pieces[0].shape[1]
    for k in range(n):
        away[:, at(lax.rem(me - k + n, n), cols)] = pieces[k][at(1 - head, half), :]


def out_term(n, *refs):
    pieces, (theirs, probe, upper, lower, total, lhs) = refs[:n], refs[n:]
    me, head = lax.axis_index("seq"), lax.axis_index("head")
    half = theirs.shape[0]
    cols = pieces[0].shape[1]
    for k in range(n):
        lhs[:, at(lax.rem(me - k + n, n), cols)] = pieces[k][at(head, half), :]
    total[...] = dot(lhs[...], probe[...])
    rows = upper.shape[0]
    total[...] += dot(theirs[:, :rows], upper[...])
    total[...] += dot(theirs[:, rows:], lower[...])


def out_sum(n, *refs):
    base, pieces, (weight, one, two, out, lhs) = refs[0], refs[1 : n + 1], refs[n + 1 :]
    me, group = lax.axis_index("seq"), lax.axis_index("groups")
    cols = pieces[0].shape[1] // 2
    for k in range(n):
        where = at(lax.rem(me - k + n, n), cols)
        for d in range(2):
            lhs[d, :, where] = pieces[k][:, d * cols : (d + 1) * cols]
    rows = one.shape[0]
    total = base[...] + dot(lhs[0], weight[...])
    total = total + dot(lhs[1, :, at(group, rows)], one[...])
    out[...] = (total + dot(lhs[1, :, at(1 - group, rows)], two[...])).astype(jnp.bfloat16)


def grad_far(n, mine, other_core, weight, one, two, tangent_out, share, out):
    me, group = lax.axis_index("seq"), lax.axis_index("groups")
    cols = out.shape[1] // 2
    tangent_out[...] = (mine[...].astype(jnp.float32) + other_core[...].astype(jnp.float32)).astype(jnp.bfloat16)
    share[...] = tangent_out[at(lax.axis_index("rep"), share.shape[0]), :]
    where = lax.rem(me + n // 2, n)
    out[:, :cols] = dot(tangent_out[...], weight[at(where, cols), :], 1, 1).astype(jnp.bfloat16)
    near = where // (n // 2) == group

    @pl.when(near)
    def _():
        rows = one[at(lax.rem(where, n // 2), cols), :]
        out[:, cols:] = dot(tangent_out[...], rows, 1, 1).astype(jnp.bfloat16)

    @pl.when(jnp.logical_not(near))
    def _():
        rows = two[at(lax.rem(where, n // 2), cols), :]
        out[:, cols:] = dot(tangent_out[...], rows, 1, 1).astype(jnp.bfloat16)


def grad_term(n, tangent_out, weight, one, two, *refs):
    outs, grad = refs[: n - 1], refs[n - 1]
    me, group = lax.axis_index("seq"), lax.axis_index("groups")
    cols = outs[0].shape[1] // 2
    rows = one.shape[0]
    grad[0] = dot(tangent_out[...], weight[...], 1, 1).astype(jnp.bfloat16)
    grad[1, :, at(group, rows)] = dot(tangent_out[...], one[...], 1, 1).astype(jnp.bfloat16)
    grad[1, :, at(1 - group, rows)] = dot(tangent_out[...], two[...], 1, 1).astype(jnp.bfloat16)
    for d in range(2):
        for j, k in enumerate(k for k in range(n) if k != n // 2):
            outs[j][:, d * cols : (d + 1) * cols] = grad[d, :, at(lax.rem(me + k, n), cols)]


def add_grad(n, *refs):
    terms, home, away = refs[:n], refs[n], refs[n + 1]
    total = terms[0][...].astype(jnp.float32)
    for term in terms[1:]:
        total = total + term[...].astype(jnp.float32)
    cols = home.shape[1]
    home[...] = total[:, :cols].astype(jnp.bfloat16)
    away[...] = total[:, cols:].astype(jnp.bfloat16)


def key_grad(mine, theirs, probs, out, grad, held, sems):
    heads, tokens, _ = probs.shape
    half, cols = mine.shape
    parts = held.shape[0]
    rows = tokens // parts
    copies = [pltpu.make_async_copy(probs.at[:, pl.ds(c * rows, rows)], held.at[c], sems.at[c]) for c in range(parts)]
    for copy in copies:
        copy.start()
    head = lax.axis_index("head")
    grad[at(head, half), :] = mine[...]
    grad[at(1 - head, half), :] = theirs[...]
    lane = lax.broadcasted_iota(jnp.int32, (rows, cols), 1) // DH
    for c in range(parts):
        copies[c].wait()
        value = dot(held[c, 0], grad[...])
        for h in range(1, heads):
            value = jnp.where(lane == h, dot(held[c, h], grad[...]), value)
        out[pl.ds(c * rows, rows), :] = value.astype(jnp.bfloat16)


def value_product(n, *refs):
    flipped, blocks, out, rhs = refs[0], refs[1 : n + 1], refs[n + 1], refs[n + 2]
    me = lax.axis_index("seq")
    cols = blocks[0].shape[1]
    for k in range(n):
        rhs[:, at(lax.rem(me - k + n, n), cols)] = blocks[k][...]
    out[...] = dot(flipped[...], rhs[...]).astype(jnp.bfloat16)


def out_product(n, *refs):
    pieces, (mine, one, two, out, rows) = refs[:n], refs[n:]
    me, head, rep = lax.axis_index("seq"), lax.axis_index("head"), lax.axis_index("rep")
    cols = pieces[0].shape[1]
    half, part = mine.shape[0], one.shape[0]
    rows[at(head, half), :] = mine[...]
    for index, piece in ((rep, one), (1 - rep, two)):
        start = (1 - head) * half + index * part
        rows[pl.ds(pl.multiple_of(start, part), part), :] = piece[...]
    for k in range(n):
        out[at(lax.rem(me - k + n, n), cols), :] = dot(pieces[k][...].T, rows[...]).astype(jnp.bfloat16)


def by_heads(normed, query_proj, key_proj, value_proj, out_weight, value_probe, out_probe):
    n = lax.axis_size("seq")
    me, head, rep = lax.axis_index("seq"), lax.axis_index("head"), lax.axis_index("rep")
    tok, width = normed.shape
    block = query_proj.shape[1]
    slab, cols, tokens = width // n, block // n, tok * n
    half, heads = tokens // 2, block // n // DH
    call = Chain()
    part = partial
    dma = pltpu.SemaphoreType.DMA
    f32 = jnp.float32

    def held(*shape):
        return pltpu.VMEM(shape, jnp.bfloat16)

    def gathered(x):
        pieces = [x] + [None] * (n - 1)
        for k in range(1, (n - 1) // 2 + 1):
            pieces[k] = ahead(pieces[k - 1], 1)
        for k in range(1, n // 2 + 1):
            pieces[n - k] = ahead(pieces[(n - k + 1) % n], n - 1)
        return pieces

    def summed(terms, together=False):
        sums = [terms[0]]
        ways = ((1, n // 2), (-1, (n - 1) // 2))
        begun = [ahead(terms[step * far], step) for step, far in ways]
        for (step, far), total in zip(ways, begun):
            for k in range(far - 1, 0, -1):
                first = begun if together else ()
                (total,) = call(add, [bf(*total.shape)], [total, terms[step * k]], first=first)
                total = ahead(total, step)
            sums.append(total)
        return sums

    quarter = tok // 4
    start = (rep * 2 + head) * quarter
    got = [
        ahead(lax.dynamic_slice(normed, (start, lax.rem(me + k, n) * slab), (quarter, slab)), k) for k in range(1, n)]
    proj = (query_proj, key_proj, value_proj)
    qkv = []
    for k in range(1, n):
        piece = jnp.stack([lax.dynamic_slice(x, (0, lax.rem(me + k, n) * cols), (tok, cols)) for x in proj])
        qkv.append(ahead(after(piece, got[0]), k))
    got = got[-1:] + got[:-1]
    other = [swap(x, "head") for x in got]
    packed, share, upper, lower = call(
        pack, [bf(2 * (n - 1), quarter, slab)] + [bf(block // 2, slab)] * 3, [*got, *other, out_weight, out_probe],
        scratch=[dma((3,))], in_specs=[VMEM] * (2 * n - 2) + [ANY] * 2, first=qkv[:2])
    feats, *terms = call(
        part(tangent_term, n), [bf(tokens, slab)] + [bf(tokens, cols)] * n,
        [normed, packed, swap(packed, "rep"), value_probe], scratch=[held(tokens, block), dma(())],
        in_specs=[ANY] + [VMEM] * 3)
    upper = swap(upper, "head")
    weights = [swap(after(share, feats), "head")]
    probs, attended = call(
        part(attend, n), [bf(heads, tokens, tokens), bf(tokens, cols)], [*proj, *qkv],
        scratch=[held(tokens, cols)] * 3, mib=32)
    att = gathered(attended)
    tangent = summed(terms, together=True)
    tan, tan_away = call(
        part(attend_tan, 3), [bf(half, cols)] * 2, [*tangent, probs],
        scratch=[held(heads, tokens, tokens), held(tokens, cols), dma((heads,))], in_specs=[VMEM] * 3 + [ANY], first=[upper])
    (tan,) = call(join, [bf(half, 2 * cols)], [tan, swap(tan_away, "head")], first=[att[1], att[-1]])
    weights.append(swap(weights[0], "groups"))
    tan = gathered(tan)
    (away,) = call(part(cut_rows, n), [bf(half, block)], att)
    lower = swap(after(lower, tan[0]), "head")
    (base,) = call(
        part(out_term, n), [jax.ShapeDtypeStruct((half, slab), f32)],
        [*att, swap(away, "head"), out_probe, upper, lower], scratch=[held(half, block)])
    (mine,) = call(
        part(out_sum, n), [bf(half, slab)], [base, *tan, out_weight, *weights], scratch=[held(2, half, block)])
    tangent_out, share, far = call(
        part(grad_far, n), [bf(half, slab), bf(half // 2, slab), bf(half, 2 * cols)],
        [mine, swap(mine, "rep"), out_weight, *weights])
    grads = call(
        part(grad_term, n), [bf(half, 2 * cols)] * (n - 1), [tangent_out, out_weight, *weights],
        scratch=[held(2, half, block)])
    grads = [*grads[: n // 2], far, *grads[n // 2 :]]
    home, away = call(part(add_grad, 3), [bf(half, cols)] * 2, summed(grads))
    (value_grad,) = call(
        key_grad, [bf(tokens, cols)], [home, swap(away, "head"), probs],
        scratch=[held(tokens, cols), held(4, heads, tokens // 4, tokens), dma((4,))], in_specs=[VMEM] * 2 + [ANY])
    value_grad = gathered(value_grad)
    share = swap(share, "head")
    (out_curv,) = call(
        part(out_product, n), [bf(block, slab)], [*att, tangent_out, share, swap(share, "rep")],
        scratch=[held(tokens, slab)])
    (flipped,) = call(flip, [bf(slab, tokens)], [feats])
    (value_curv,) = call(
        part(value_product, n), [bf(slab, block)], [flipped, *value_grad], scratch=[held(tokens, block)])
    return value_curv, out_curv


def body(*args):
    tok, cols = args[1].shape
    n = lax.axis_size("seq")
    even = n % 2 == 0 and cols % (n * 128) == 0 and tok % 64 == 0 and tok * n % 64 == 0
    if even and all(lax.axis_size(axis) == 2 for axis in ("groups", "head", "rep")):
        return by_heads(*args)
    return by_tokens(*args)


def by_tokens(normed, query_proj, key_proj, value_proj, out_weight, value_probe, out_probe):
    tok_rows = normed.shape[0]
    col_count = query_proj.shape[1]
    local_heads = col_count // DH
    feature_cols = normed
    value_tangent = jnp.dot(
        feature_cols,
        lax.all_gather(value_probe, "seq", axis=0, tiled=True),
        preferred_element_type=jnp.float32,
    ).astype(jnp.bfloat16)
    query_heads = query_proj.reshape(tok_rows, local_heads, DH)
    run_max = jnp.full((tok_rows, local_heads), -1e30, jnp.float32)
    key_rows = lax.all_gather(key_proj, "seq", axis=0, tiled=True)
    value_rows = lax.all_gather(value_proj, "seq", axis=0, tiled=True)
    tangent_rows = lax.all_gather(value_tangent, "seq", axis=0, tiled=True)
    piece_rows = key_rows.shape[0]
    key_heads = key_rows.reshape(piece_rows, local_heads, DH)
    value_heads = value_rows.reshape(piece_rows, local_heads, DH)
    tangent_heads = tangent_rows.reshape(piece_rows, local_heads, DH)
    scores = jnp.einsum("qhd,khd->qhk", query_heads, key_heads, preferred_element_type=jnp.float32)
    next_max = jnp.maximum(run_max, jnp.max(scores, axis=2))
    exp_rows = jnp.exp(scores - next_max[:, :, None])
    run_sum = jnp.sum(exp_rows, axis=2)
    prob_bf = exp_rows.astype(jnp.bfloat16)
    accum_v = jnp.einsum("qhk,khd->qhd", prob_bf, value_heads, preferred_element_type=jnp.float32)
    accum_t = jnp.einsum("qhk,khd->qhd", prob_bf, tangent_heads, preferred_element_type=jnp.float32)
    run_max, run_sum, accum_v, accum_t = (next_max, run_sum, accum_v, accum_t)
    row_lse = run_max + jnp.log(run_sum)
    attended = (accum_v / run_sum[:, :, None]).reshape(tok_rows, col_count).astype(jnp.bfloat16)
    attended_tan = (accum_t / run_sum[:, :, None]).reshape(tok_rows, col_count).astype(jnp.bfloat16)
    weight_full, probe_full = (
        lax.all_gather(out_weight, "seq", axis=1, tiled=True),
        lax.all_gather(out_probe, "seq", axis=1, tiled=True),
    )
    partial_out = jnp.dot(attended_tan, weight_full, preferred_element_type=jnp.float32) + jnp.dot(
        attended, probe_full, preferred_element_type=jnp.float32
    )
    tangent_out = lax.psum(partial_out.astype(jnp.bfloat16), ("head", "rep"))
    out_term = jnp.einsum("tc,td->cd", attended, tangent_out, preferred_element_type=jnp.float32)
    out_curv = lax.psum_scatter(
        out_term.astype(jnp.bfloat16), "seq", scatter_dimension=1, tiled=True
    )
    grad_out = jnp.einsum(
        "td,cd->tc", tangent_out, weight_full, preferred_element_type=jnp.float32
    ).astype(jnp.bfloat16)
    grad_heads = grad_out.reshape(tok_rows, local_heads, DH)
    every_key = lax.all_gather(key_proj, "seq", axis=0, tiled=True)
    key_rows = every_key.reshape(tok_rows * lax.axis_size("seq"), local_heads, DH)
    scores = jnp.einsum("qhd,khd->qhk", query_heads, key_rows, preferred_element_type=jnp.float32)
    prob_bf = jnp.exp(scores - row_lse[:, :, None]).astype(jnp.bfloat16)
    value_grad = lax.psum_scatter(
        jnp.einsum("qhk,qhd->khd", prob_bf, grad_heads, preferred_element_type=jnp.float32)
        .reshape(tok_rows * lax.axis_size("seq"), col_count)
        .astype(jnp.bfloat16),
        "seq",
        scatter_dimension=0,
        tiled=True,
    )
    feature_cols = normed
    value_curv = lax.psum_scatter(
        jnp.einsum(
            "tr,tc->rc", feature_cols, value_grad, preferred_element_type=jnp.float32
        ).astype(jnp.bfloat16),
        "seq",
        scatter_dimension=0,
        tiled=True,
    )
    return (value_curv, out_curv)


def solution(mesh):
    in_specs = (
        P(("groups", "seq"), None),
        P(("groups", "seq"), ("head", "rep")),
        P(("groups", "seq"), ("head", "rep")),
        P(("groups", "seq"), ("head", "rep")),
        P(("head", "rep"), "seq"),
        P(("groups", "seq"), ("head", "rep")),
        P(("groups", "head", "rep"), "seq"),
    )
    out_specs = (P(("groups", "seq"), ("head", "rep")), P(("groups", "head", "rep"), "seq"))
    return jax.shard_map(body, mesh=mesh, in_specs=in_specs, out_specs=out_specs, check_vma=False)
```

```python
from functools import partial

import jax
import jax.numpy as jnp
from jax import lax
from jax.experimental import pallas as pl
from jax.experimental.pallas import tpu as pltpu
from jax.sharding import PartitionSpec as P

DH = 64


VMEM = pl.BlockSpec(memory_space=pltpu.VMEM)
HBM = pl.BlockSpec(memory_space=pltpu.HBM)
ANY = pl.BlockSpec(memory_space=pl.ANY)


class Chain:
    def __init__(self):
        self.last = None

    def __call__(self, kernel, outs, ins, scratch=(), in_specs=None, first=(), mib=18):
        specs = in_specs or [VMEM] * len(ins)
        out_specs = [HBM] * len(outs) if in_specs and HBM in in_specs and VMEM not in in_specs else [VMEM] * len(outs)
        count = len(ins)
        if self.last is not None:
            first = [*first, self.last]
        ins, specs = [*ins, *first], [*specs, *[ANY] * len(first)]

        def body(*refs):
            kernel(*refs[:count], *refs[len(ins) :])

        results = pl.pallas_call(
            body,
            out_shape=outs,
            in_specs=specs,
            out_specs=out_specs,
            scratch_shapes=list(scratch),
            compiler_params=pltpu.CompilerParams(vmem_limit_bytes=mib * 2**20),
            cost_estimate=pl.CostEstimate(flops=1, bytes_accessed=1, transcendentals=0),
            name=getattr(kernel, "func", kernel).__name__,
        )(*ins)
        self.last = results[0]
        return results


def bf(*shape):
    return jax.ShapeDtypeStruct(shape, jnp.bfloat16)


def dot(a, b, ca=1, cb=0):
    return lax.dot_general(a, b, (((ca,), (cb,)), ((), ())), preferred_element_type=jnp.float32)


def at(index, size):
    return pl.ds(pl.multiple_of(index * size, size), size)


def ahead(x, k):
    n = lax.axis_size("seq")
    return lax.ppermute(x, "seq", [(i, (i + k) % n) for i in range(n)])


def swap(x, axis):
    return lax.ppermute(x, axis, [(0, 1), (1, 0)])


def after(x, *first):
    return lax.optimization_barrier((x, *first))[0]


def pack(*refs):
    *pieces, weight, probe, out, share, upper, lower, sems = refs
    rows = share.shape[0]
    copies = [
        pltpu.make_async_copy(weight.at[at(lax.axis_index("groups"), rows)], share, sems.at[0]),
        pltpu.make_async_copy(probe.at[pl.ds(0, rows)], upper, sems.at[1]),
        pltpu.make_async_copy(probe.at[pl.ds(rows, rows)], lower, sems.at[2]),
    ]
    for copy in copies:
        copy.start()
    for j, piece in enumerate(pieces):
        out[j] = piece[...]
    for copy in copies:
        copy.wait()


def tangent_term(n, normed, packed, peer, probe, feats, *refs):
    outs, whole, sem = refs[:n], refs[n], refs[n + 1]
    me, head, rep = lax.axis_index("seq"), lax.axis_index("head"), lax.axis_index("rep")
    tok = normed.shape[0]
    part, slab = packed.shape[1:]
    copy = pltpu.make_async_copy(normed.at[:, at(me, slab)], feats.at[at(me, tok)], sem)
    copy.start()
    cols = outs[0].shape[1]
    for k in [*range(1, n), 0]:
        block = lax.rem(me - k + n, n)
        if k == 0:
            copy.wait()
        else:
            for rows, core in ((packed, rep), (peer, 1 - rep)):
                for row, side in ((k % (n - 1), head), (n - 1 + k % (n - 1), 1 - head)):
                    start = block * tok + (core * 2 + side) * part
                    feats[pl.ds(pl.multiple_of(start, part), part), :] = rows[row]
        whole[at(block, tok), :] = dot(feats[at(block, tok), :], probe[...]).astype(jnp.bfloat16)
    for k in range(n):
        outs[k][...] = whole[:, at(lax.rem(me + k, n), cols)]


def flip(feats, out):
    out[...] = feats[...].T


def keep_heads(parts):
    return jnp.concatenate([part[h * DH : (h + 1) * DH] for h, part in enumerate(parts)], axis=0)


def attend(n, *refs):
    own, pieces, (probs, attended, *all3) = refs[:3], refs[3 : n + 2], refs[n + 2 :]
    q_all, k_all, v_all = all3
    me = lax.axis_index("seq")
    tok, cols = pieces[0].shape[1:]
    for j in range(3):
        all3[j][at(me, tok), :] = own[j][:, at(me, cols)]
        for k in range(1, n):
            all3[j][at(lax.rem(me - k + n, n), tok), :] = pieces[k - 1][j]
    heads = cols // DH
    v_flip = v_all[...].T
    step = probs.shape[2] // 2
    lane = lax.broadcasted_iota(jnp.int32, (step, cols), 1) // DH
    for c in range(2):
        rows = slice(c * step, (c + 1) * step)
        scores = [dot(k_all[...], jnp.where(lane == h, q_all[rows, :], 0), 1, 1) for h in range(heads)]
        parts = []
        for h in range(heads):
            exps = jnp.exp(scores[h] - jnp.max(scores[h], axis=0, keepdims=True))
            prob = (exps * (1.0 / jnp.sum(exps, axis=0, keepdims=True))).astype(jnp.bfloat16)
            probs[h, :, rows] = prob
            parts.append(dot(v_flip, prob))
        attended[rows, :] = keep_heads(parts).T.astype(jnp.bfloat16)


def halves(rows, home, away):
    head = lax.axis_index("head")
    half = home.shape[0]
    home[...] = rows[at(head, half), :]
    away[...] = rows[at(1 - head, half), :]


def attend_tan(n, *refs):
    terms, probs, (home, away, held, result, sems) = refs[:n], refs[n], refs[n + 1 :]
    heads = probs.shape[0]
    copies = [pltpu.make_async_copy(probs.at[h], held.at[h], sems.at[h]) for h in range(heads)]
    for copy in copies:
        copy.start()
    total = terms[0][...].astype(jnp.float32)
    for term in terms[1:]:
        total = total + term[...].astype(jnp.float32)
    flipped = total.T.astype(jnp.bfloat16)
    parts = []
    for h in range(heads):
        copies[h].wait()
        parts.append(dot(flipped, held[h]))
    result[...] = keep_heads(parts).T.astype(jnp.bfloat16)
    halves(result, home, away)


def add(one, two, out):
    out[...] = (one[...].astype(jnp.float32) + two[...].astype(jnp.float32)).astype(jnp.bfloat16)


def join(home, other, out):
    cols = home.shape[1]
    out[:, :cols] = home[...]
    out[:, cols:] = other[...]


def cut_rows(n, *refs):
    pieces, away = refs[:n], refs[n]
    me, head = lax.axis_index("seq"), lax.axis_index("head")
    half = away.shape[0]
    cols = pieces[0].shape[1]
    for k in range(n):
        away[:, at(lax.rem(me - k + n, n), cols)] = pieces[k][at(1 - head, half), :]


def out_term(n, *refs):
    pieces, (theirs, probe, upper, lower, total, lhs) = refs[:n], refs[n:]
    me, head = lax.axis_index("seq"), lax.axis_index("head")
    half = theirs.shape[0]
    cols = pieces[0].shape[1]
    for k in range(n):
        lhs[:, at(lax.rem(me - k + n, n), cols)] = pieces[k][at(head, half), :]
    total[...] = dot(lhs[...], probe[...])
    rows = upper.shape[0]
    total[...] += dot(theirs[:, :rows], upper[...])
    total[...] += dot(theirs[:, rows:], lower[...])


def out_sum(n, *refs):
    base, pieces, (weight, one, two, out, lhs) = refs[0], refs[1 : n + 1], refs[n + 1 :]
    me, group = lax.axis_index("seq"), lax.axis_index("groups")
    cols = pieces[0].shape[1] // 2
    for k in range(n):
        where = at(lax.rem(me - k + n, n), cols)
        for d in range(2):
            lhs[d, :, where] = pieces[k][:, d * cols : (d + 1) * cols]
    rows = one.shape[0]
    total = base[...] + dot(lhs[0], weight[...])
    total = total + dot(lhs[1, :, at(group, rows)], one[...])
    out[...] = (total + dot(lhs[1, :, at(1 - group, rows)], two[...])).astype(jnp.bfloat16)


def grad_far(n, mine, other_core, weight, one, two, tangent_out, share, out):
    me, group = lax.axis_index("seq"), lax.axis_index("groups")
    cols = out.shape[1] // 2
    tangent_out[...] = (mine[...].astype(jnp.float32) + other_core[...].astype(jnp.float32)).astype(jnp.bfloat16)
    share[...] = tangent_out[at(lax.axis_index("rep"), share.shape[0]), :]
    where = lax.rem(me + n // 2, n)
    out[:, :cols] = dot(tangent_out[...], weight[at(where, cols), :], 1, 1).astype(jnp.bfloat16)
    near = where // (n // 2) == group

    @pl.when(near)
    def _():
        rows = one[at(lax.rem(where, n // 2), cols), :]
        out[:, cols:] = dot(tangent_out[...], rows, 1, 1).astype(jnp.bfloat16)

    @pl.when(jnp.logical_not(near))
    def _():
        rows = two[at(lax.rem(where, n // 2), cols), :]
        out[:, cols:] = dot(tangent_out[...], rows, 1, 1).astype(jnp.bfloat16)


def grad_term(n, tangent_out, weight, one, two, *refs):
    outs, grad = refs[: n - 1], refs[n - 1]
    me, group = lax.axis_index("seq"), lax.axis_index("groups")
    cols = outs[0].shape[1] // 2
    rows = one.shape[0]
    grad[0] = dot(tangent_out[...], weight[...], 1, 1).astype(jnp.bfloat16)
    grad[1, :, at(group, rows)] = dot(tangent_out[...], one[...], 1, 1).astype(jnp.bfloat16)
    grad[1, :, at(1 - group, rows)] = dot(tangent_out[...], two[...], 1, 1).astype(jnp.bfloat16)
    for d in range(2):
        for j, k in enumerate(k for k in range(n) if k != n // 2):
            outs[j][:, d * cols : (d + 1) * cols] = grad[d, :, at(lax.rem(me + k, n), cols)]


def add_grad(n, *refs):
    terms, home, away = refs[:n], refs[n], refs[n + 1]
    total = terms[0][...].astype(jnp.float32)
    for term in terms[1:]:
        total = total + term[...].astype(jnp.float32)
    cols = home.shape[1]
    home[...] = total[:, :cols].astype(jnp.bfloat16)
    away[...] = total[:, cols:].astype(jnp.bfloat16)


def key_grad(part, *refs):
    if part:
        base, *refs = refs
    piece, probs, out, held, sems = refs
    heads, tokens, _ = probs.shape
    half, cols = piece.shape
    parts = held.shape[0]
    rows = tokens // parts
    head = lax.axis_index("head")
    queries = at(1 - head if part else head, half)
    copies = [
        pltpu.make_async_copy(probs.at[:, pl.ds(c * rows, rows), queries], held.at[c], sems.at[c])
        for c in range(parts)]
    for copy in copies:
        copy.start()
    lane = lax.broadcasted_iota(jnp.int32, (rows, cols), 1) // DH
    for c in range(parts):
        copies[c].wait()
        value = dot(held[c, 0], piece[...])
        for h in range(1, heads):
            value = jnp.where(lane == h, dot(held[c, h], piece[...]), value)
        if part:
            value = value + base[c * rows : (c + 1) * rows, :]
        out[c * rows : (c + 1) * rows, :] = value.astype(out.dtype)


def value_part(*refs):
    count = len(refs) // 2
    flipped, blocks, outs = refs[0], refs[1 : count + 1], refs[count + 1 :]
    for block, out in zip(blocks, outs):
        out[...] = dot(flipped[...], block[...]).astype(jnp.bfloat16)


def value_product(n, *refs):
    flipped, block, parts, out = refs[0], refs[1], refs[2 : n + 1], refs[n + 1]
    me = lax.axis_index("seq")
    cols = block.shape[1]
    for k, part in zip((k for k in range(n) if k != n // 2), parts):
        out[:, at(lax.rem(me - k + n, n), cols)] = part[...]
    where = at(lax.rem(me - n // 2 + n, n), cols)
    out[:, where] = dot(flipped[...], block[...]).astype(jnp.bfloat16)


def out_product(n, *refs):
    pieces, (mine, one, two, out, rows) = refs[:n], refs[n:]
    me, head, rep = lax.axis_index("seq"), lax.axis_index("head"), lax.axis_index("rep")
    cols = pieces[0].shape[1]
    half, part = mine.shape[0], one.shape[0]
    rows[at(head, half), :] = mine[...]
    for index, piece in ((rep, one), (1 - rep, two)):
        start = (1 - head) * half + index * part
        rows[pl.ds(pl.multiple_of(start, part), part), :] = piece[...]
    for k in range(n):
        out[at(lax.rem(me - k + n, n), cols), :] = dot(pieces[k][...].T, rows[...]).astype(jnp.bfloat16)


def by_heads(normed, query_proj, key_proj, value_proj, out_weight, value_probe, out_probe):
    n = lax.axis_size("seq")
    me, head, rep = lax.axis_index("seq"), lax.axis_index("head"), lax.axis_index("rep")
    tok, width = normed.shape
    block = query_proj.shape[1]
    slab, cols, tokens = width // n, block // n, tok * n
    half, heads = tokens // 2, block // n // DH
    call = Chain()
    part = partial
    dma = pltpu.SemaphoreType.DMA
    f32 = jnp.float32

    def held(*shape):
        return pltpu.VMEM(shape, jnp.bfloat16)

    def gathered(x):
        pieces = [x] + [None] * (n - 1)
        for k in range(1, (n - 1) // 2 + 1):
            pieces[k] = ahead(pieces[k - 1], 1)
        for k in range(1, n // 2 + 1):
            pieces[n - k] = ahead(pieces[(n - k + 1) % n], n - 1)
        return pieces

    def summed(terms, together=False):
        sums = [terms[0]]
        ways = ((1, n // 2), (-1, (n - 1) // 2))
        begun = [ahead(terms[step * far], step) for step, far in ways]
        for (step, far), total in zip(ways, begun):
            for k in range(far - 1, 0, -1):
                first = begun if together else ()
                (total,) = call(add, [bf(*total.shape)], [total, terms[step * k]], first=first)
                total = ahead(total, step)
            sums.append(total)
        return sums

    quarter = tok // 4
    start = (rep * 2 + head) * quarter
    got = [
        ahead(lax.dynamic_slice(normed, (start, lax.rem(me + k, n) * slab), (quarter, slab)), k) for k in range(1, n)]
    proj = (query_proj, key_proj, value_proj)
    qkv = []
    for k in range(1, n):
        piece = jnp.stack([lax.dynamic_slice(x, (0, lax.rem(me + k, n) * cols), (tok, cols)) for x in proj])
        qkv.append(ahead(after(piece, got[0]), k))
    got = got[-1:] + got[:-1]
    other = [swap(x, "head") for x in got]
    packed, share, upper, lower = call(
        pack, [bf(2 * (n - 1), quarter, slab)] + [bf(block // 2, slab)] * 3, [*got, *other, out_weight, out_probe],
        scratch=[dma((3,))], in_specs=[VMEM] * (2 * n - 2) + [ANY] * 2, first=qkv[:2])
    feats, *terms = call(
        part(tangent_term, n), [bf(tokens, slab)] + [bf(tokens, cols)] * n,
        [normed, packed, swap(packed, "rep"), value_probe], scratch=[held(tokens, block), dma(())],
        in_specs=[ANY] + [VMEM] * 3)
    upper = swap(upper, "head")
    weights = [swap(after(share, feats), "head")]
    probs, attended = call(
        part(attend, n), [bf(heads, tokens, tokens), bf(tokens, cols)], [*proj, *qkv],
        scratch=[held(tokens, cols)] * 3, mib=32)
    att = gathered(attended)
    tangent = summed(terms, together=True)
    tan, tan_away = call(
        part(attend_tan, 3), [bf(half, cols)] * 2, [*tangent, probs],
        scratch=[held(heads, tokens, tokens), held(tokens, cols), dma((heads,))], in_specs=[VMEM] * 3 + [ANY], first=[upper])
    (tan,) = call(join, [bf(half, 2 * cols)], [tan, swap(tan_away, "head")], first=[att[1], att[-1]])
    weights.append(swap(weights[0], "groups"))
    tan = gathered(tan)
    (away,) = call(part(cut_rows, n), [bf(half, block)], att)
    lower = swap(after(lower, tan[0]), "head")
    (base,) = call(
        part(out_term, n), [jax.ShapeDtypeStruct((half, slab), f32)],
        [*att, swap(away, "head"), out_probe, upper, lower], scratch=[held(half, block)])
    (mine,) = call(
        part(out_sum, n), [bf(half, slab)], [base, *tan, out_weight, *weights], scratch=[held(2, half, block)])
    tangent_out, share, far = call(
        part(grad_far, n), [bf(half, slab), bf(half // 2, slab), bf(half, 2 * cols)],
        [mine, swap(mine, "rep"), out_weight, *weights])
    grads = call(
        part(grad_term, n), [bf(half, 2 * cols)] * (n - 1), [tangent_out, out_weight, *weights],
        scratch=[held(2, half, block)])
    grads = [*grads[: n // 2], far, *grads[n // 2 :]]
    home, away = call(part(add_grad, 3), [bf(half, cols)] * 2, summed(grads))
    value_grad = None
    for j, piece in enumerate((home, swap(away, "head"))):
        (value_grad,) = call(
            part(key_grad, j), [jax.ShapeDtypeStruct((tokens, cols), jnp.bfloat16 if j else f32)],
            [value_grad, piece, probs] if j else [piece, probs],
            scratch=[held(4, heads, tokens // 4, half), dma((4,))], in_specs=[VMEM] * (j + 1) + [ANY])
    value_grad = gathered(value_grad)
    share = swap(share, "head")
    (out_curv,) = call(
        part(out_product, n), [bf(block, slab)], [*att, tangent_out, share, swap(share, "rep")],
        scratch=[held(tokens, slab)])
    (flipped,) = call(flip, [bf(slab, tokens)], [feats])
    far = value_grad.pop(n // 2)
    parts = call(value_part, [bf(slab, cols)] * (n - 1), [flipped, *value_grad])
    (value_curv,) = call(part(value_product, n), [bf(slab, block)], [flipped, far, *parts])
    return value_curv, out_curv


def body(*args):
    tok, cols = args[1].shape
    n = lax.axis_size("seq")
    even = n % 2 == 0 and cols % (n * 128) == 0 and tok % 64 == 0 and tok * n % 64 == 0
    if even and all(lax.axis_size(axis) == 2 for axis in ("groups", "head", "rep")):
        return by_heads(*args)
    return by_tokens(*args)


def by_tokens(normed, query_proj, key_proj, value_proj, out_weight, value_probe, out_probe):
    tok_rows = normed.shape[0]
    col_count = query_proj.shape[1]
    local_heads = col_count // DH
    feature_cols = normed
    value_tangent = jnp.dot(
        feature_cols,
        lax.all_gather(value_probe, "seq", axis=0, tiled=True),
        preferred_element_type=jnp.float32,
    ).astype(jnp.bfloat16)
    query_heads = query_proj.reshape(tok_rows, local_heads, DH)
    run_max = jnp.full((tok_rows, local_heads), -1e30, jnp.float32)
    key_rows = lax.all_gather(key_proj, "seq", axis=0, tiled=True)
    value_rows = lax.all_gather(value_proj, "seq", axis=0, tiled=True)
    tangent_rows = lax.all_gather(value_tangent, "seq", axis=0, tiled=True)
    piece_rows = key_rows.shape[0]
    key_heads = key_rows.reshape(piece_rows, local_heads, DH)
    value_heads = value_rows.reshape(piece_rows, local_heads, DH)
    tangent_heads = tangent_rows.reshape(piece_rows, local_heads, DH)
    scores = jnp.einsum("qhd,khd->qhk", query_heads, key_heads, preferred_element_type=jnp.float32)
    next_max = jnp.maximum(run_max, jnp.max(scores, axis=2))
    exp_rows = jnp.exp(scores - next_max[:, :, None])
    run_sum = jnp.sum(exp_rows, axis=2)
    prob_bf = exp_rows.astype(jnp.bfloat16)
    accum_v = jnp.einsum("qhk,khd->qhd", prob_bf, value_heads, preferred_element_type=jnp.float32)
    accum_t = jnp.einsum("qhk,khd->qhd", prob_bf, tangent_heads, preferred_element_type=jnp.float32)
    run_max, run_sum, accum_v, accum_t = (next_max, run_sum, accum_v, accum_t)
    row_lse = run_max + jnp.log(run_sum)
    attended = (accum_v / run_sum[:, :, None]).reshape(tok_rows, col_count).astype(jnp.bfloat16)
    attended_tan = (accum_t / run_sum[:, :, None]).reshape(tok_rows, col_count).astype(jnp.bfloat16)
    weight_full, probe_full = (
        lax.all_gather(out_weight, "seq", axis=1, tiled=True),
        lax.all_gather(out_probe, "seq", axis=1, tiled=True),
    )
    partial_out = jnp.dot(attended_tan, weight_full, preferred_element_type=jnp.float32) + jnp.dot(
        attended, probe_full, preferred_element_type=jnp.float32
    )
    tangent_out = lax.psum(partial_out.astype(jnp.bfloat16), ("head", "rep"))
    out_term = jnp.einsum("tc,td->cd", attended, tangent_out, preferred_element_type=jnp.float32)
    out_curv = lax.psum_scatter(
        out_term.astype(jnp.bfloat16), "seq", scatter_dimension=1, tiled=True
    )
    grad_out = jnp.einsum(
        "td,cd->tc", tangent_out, weight_full, preferred_element_type=jnp.float32
    ).astype(jnp.bfloat16)
    grad_heads = grad_out.reshape(tok_rows, local_heads, DH)
    every_key = lax.all_gather(key_proj, "seq", axis=0, tiled=True)
    key_rows = every_key.reshape(tok_rows * lax.axis_size("seq"), local_heads, DH)
    scores = jnp.einsum("qhd,khd->qhk", query_heads, key_rows, preferred_element_type=jnp.float32)
    prob_bf = jnp.exp(scores - row_lse[:, :, None]).astype(jnp.bfloat16)
    value_grad = lax.psum_scatter(
        jnp.einsum("qhk,qhd->khd", prob_bf, grad_heads, preferred_element_type=jnp.float32)
        .reshape(tok_rows * lax.axis_size("seq"), col_count)
        .astype(jnp.bfloat16),
        "seq",
        scatter_dimension=0,
        tiled=True,
    )
    feature_cols = normed
    value_curv = lax.psum_scatter(
        jnp.einsum(
            "tr,tc->rc", feature_cols, value_grad, preferred_element_type=jnp.float32
        ).astype(jnp.bfloat16),
        "seq",
        scatter_dimension=0,
        tiled=True,
    )
    return (value_curv, out_curv)


def solution(mesh):
    in_specs = (
        P(("groups", "seq"), None),
        P(("groups", "seq"), ("head", "rep")),
        P(("groups", "seq"), ("head", "rep")),
        P(("groups", "seq"), ("head", "rep")),
        P(("head", "rep"), "seq"),
        P(("groups", "seq"), ("head", "rep")),
        P(("groups", "head", "rep"), "seq"),
    )
    out_specs = (P(("groups", "seq"), ("head", "rep")), P(("groups", "head", "rep"), "seq"))
    return jax.shard_map(body, mesh=mesh, in_specs=in_specs, out_specs=out_specs, check_vma=False)
```
